128 devices in a mesh: sx: 8 (over z, core), sy: 8 (over y, x_lo), sample: 2 (over x_hi).
Axes of the slice: x: 4 (x_hi: 2, x_lo: 2; x = x_hi * 2 + x_lo), y: 4, z: 4, core: 2. Of those that a mesh axis runs over, the one named last changes fastest.
Arguments:
- inputs: bfloat16 [2, 192, 2, 128, 1024], P('sample', None, None, 'sx', 'sy'), may hold values from -6 to 6
- cotangent: bfloat16 [2, 192, 2, 128, 1024], P('sample', None, None, 'sx', 'sy'), may hold values from -6 to 6
- depth_kernel: float32 [192, 27], replicated, may hold values from -1.25 to 1.25
- mix_in: bfloat16 [192, 192], replicated, may hold values from -0.4375 to 0.4375
- mix_bias: float32 [192], replicated, may hold values from -3 to 3
- mix_out: bfloat16 [192, 192], replicated, may hold values from -0.4375 to 0.4375
Outputs:
- input_grad: bfloat16 [2, 192, 2, 128, 1024], P('sample', None, None, 'sx', 'sy')
- kernel_grad: float32 [192, 27], replicated
- mix_in_grad: float32 [192, 192], replicated
- bias_grad: float32 [192], replicated
- mix_out_grad: float32 [192, 192], replicated
The draws below stay inside these ranges and needn't reach their ends.
All inputs are finite; a program needn't handle non-finite values.
Results may differ from the reference program's by a relative error of at most 0.008.
Values may be sent and summed in bfloat16 or wider, within the bound.
A program may use at most 64 MiB of HBM per device.

```python
import math
import jax
import jax.numpy as jnp
from jax import lax

C = 192
Z = 2
RUNS = 2
NX = 128
NY = 1024


def level_of(rng, shape, split, least, high):
    def one(axis_at, parts):
        steps = jax.random.uniform(jax.random.fold_in(jax.random.fold_in(rng, 6), axis_at), (parts,), jnp.float32, least / len(split), high / len(split))
        return jnp.repeat(jnp.exp(steps), shape[axis_at] // parts).reshape((-1,) + (1,) * (len(shape) - axis_at - 1))

    factor_of = one(*split[0])
    for cut in split[1:]:
        factor_of = factor_of * one(*cut)
    return factor_of


def noise(key, dims, deviation, bound, cuts=(), held_as=jnp.bfloat16):
    loudness = level_of(key, dims, cuts, -0.22, 0.18) if cuts else 1.0
    entries = jax.random.normal(key, dims, jnp.float32) * deviation * loudness
    return jnp.minimum(jnp.maximum(entries, -bound), bound).astype(held_as)


def setup_inputs(seed: int = 0) -> dict:
    splits = jax.random.split(jax.random.key(seed), 7)
    return {
        "inputs": noise(splits[0], (RUNS, C, Z, NX, NY), 1.0, 6.0, ((0, 2), (3, 8), (4, 8))),
        "cotangent": noise(splits[1], (RUNS, C, Z, NX, NY), 1.0, 6.0, ((0, 2), (3, 8), (4, 8))),
        "depth_kernel": noise(splits[2], (C, 27), 27 ** -0.5, 1.25, (), jnp.float32),
        "mix_in": noise(splits[3], (C, C), C ** -0.5, 0.4375),
        "mix_bias": noise(splits[4], (C,), 0.5, 3.0, (), jnp.float32),
        "mix_out": noise(splits[5], (C, C), C ** -0.5, 0.4375),
    }


INV_SQRT2 = 0.7071067811865476
INV_SQRT2PI = 0.3989422804014327

def tap_list():
    listing = []
    for plane_step in (-1, 0, 1):
        for row_step in (-1, 0, 1):
            for col_step in (-1, 0, 1):
                tap_index = 9 * (plane_step + 1) + 3 * (row_step + 1) + (col_step + 1)
                listing.append((tap_index, plane_step, row_step, col_step))
    return listing

def window(padded, plane_step, row_step, col_step, sign):
    planes = padded.shape[-3] - 2
    rows = padded.shape[-2] - 2
    cols = padded.shape[-1] - 2
    start_p = 1 + sign * plane_step
    start_r = 1 + sign * row_step
    start_c = 1 + sign * col_step
    return padded[..., start_p:start_p + planes, start_r:start_r + rows, start_c:start_c + cols]

def stencil(padded, kernel, sign):
    total = None
    for tap_index, plane_step, row_step, col_step in tap_list():
        piece = window(padded, plane_step, row_step, col_step, sign)
        weight = kernel[:, tap_index].reshape(kernel.shape[0], 1, 1, 1)
        term = weight * piece.astype(jnp.float32)
        total = term if total is None else total + term
    return total

def pad_three(field):
    return jnp.pad(field, ((0, 0), (1, 1), (1, 1), (1, 1)))

def gelu_parts(pre):
    cdf = 0.5 * (1.0 + lax.erf(pre * INV_SQRT2))
    dens = jnp.exp(-0.5 * pre * pre) * INV_SQRT2PI
    return (cdf, cdf + pre * dens)

def reference(inputs, cotangent, depth_kernel, mix_in, mix_bias, mix_out):
    mix_in_f = mix_in.astype(jnp.float32)
    mix_out_f = mix_out.astype(jnp.float32)

    def one_run(carry, pair):
        field, grad_out = pair
        padded = pad_three(field)
        hidden = stencil(padded, depth_kernel, 1).astype(jnp.bfloat16)
        pre = jnp.einsum('oc,czxy->ozxy', mix_in_f, hidden.astype(jnp.float32)) + mix_bias.reshape(-1, 1, 1, 1)
        cdf, slope = gelu_parts(pre)
        act = (pre * cdf).astype(jnp.bfloat16)
        grad_f = grad_out.astype(jnp.float32)
        out_sum = jnp.einsum('ozxy,czxy->oc', grad_f, act.astype(jnp.float32))
        act_grad = jnp.einsum('oc,ozxy->czxy', mix_out_f, grad_f)
        pre_grad = (act_grad * slope).astype(jnp.bfloat16)
        pre_f = pre_grad.astype(jnp.float32)
        bias_sum = lax.optimization_barrier(jnp.sum(pre_f, axis=(1, 2, 3)))
        in_sum = jnp.einsum('ozxy,czxy->oc', pre_f, hidden.astype(jnp.float32))
        hidden_grad = jnp.einsum('oc,ozxy->czxy', mix_in_f, pre_f).astype(jnp.bfloat16)
        hidden_gf = hidden_grad.astype(jnp.float32)
        columns = [None] * 27
        for tap_index, plane_step, row_step, col_step in tap_list():
            piece = window(padded, plane_step, row_step, col_step, 1).astype(jnp.float32)
            columns[tap_index] = lax.optimization_barrier(jnp.sum(hidden_gf * piece, axis=(1, 2, 3)))
        kern_sum = jnp.stack(columns, axis=1)
        field_grad = (grad_f + stencil(pad_three(hidden_grad), depth_kernel, -1)).astype(jnp.bfloat16)
        carry = (carry[0] + kern_sum, carry[1] + in_sum, carry[2] + bias_sum, carry[3] + out_sum)
        return (carry, field_grad)
    start = (jnp.zeros((C, 27), jnp.float32), jnp.zeros((C, C), jnp.float32), jnp.zeros((C,), jnp.float32), jnp.zeros((C, C), jnp.float32))
    sums, input_grad = lax.scan(one_run, start, (inputs, cotangent))
    factor = 1.0 / math.sqrt(RUNS * Z * NX * NY)
    return (input_grad, sums[0] * factor, sums[1] * factor, sums[2] * factor, sums[3] * factor)
```

```python
import functools
import math

import jax
import jax.numpy as jnp
from jax import lax
from jax.experimental import pallas as pl
from jax.experimental.pallas import tpu as pltpu
from jax.sharding import PartitionSpec as P

INV_SQRT2 = 0.7071067811865476
INV_SQRT2PI = 0.3989422804014327
MESH = pl.DeviceIdType.MESH
F32 = jnp.float32
BF16 = jnp.bfloat16

CH = 192
NR = 16
NC = 128
RR = NR + 2
BLK = 8
CHUNK = 48


def dot(a, b):
    return jnp.dot(a, b, preferred_element_type=F32)


def dot_nt(a, b):
    return lax.dot_general(a, b, (((1,), (1,)), ((), ())), preferred_element_type=F32)


def iota(shape, dim):
    return lax.broadcasted_iota(jnp.int32, shape, dim)


def one_hot(cond):
    return jnp.where(cond, 1.0, 0.0).astype(BF16)


def pack_matrix(i):
    k = iota((2 * NC, 128), 0)
    lane = iota((2 * NC, 128), 1)
    z = k // NC
    j = k - z * NC
    at = z * RR + i + 1
    return one_hot(((j == NC - 1) & (lane == at)) | ((j == 0) & (lane == 64 + at)))


def rim_matrix(at):
    lane = iota((128, 2 * NC), 0)
    j = iota((128, 2 * NC), 1)
    return one_hot(((j == 0) & (lane == at)) | ((j == 2 * NC - 1) & (lane == 64 + at)))


def shift_matrix():
    k = iota((NC, 2 * NC), 0)
    j = iota((NC, 2 * NC), 1)
    return one_hot(((j < NC) & (k == j - 1)) | ((j >= NC) & (k == j - NC + 1)))


def stencil_block(a0, am, ap, w, flip, rows, emit):
    k0 = [w[8 - t if flip else t, rows, :] for t in range(9)]
    kp = [w[18 + 8 - t if flip else 9 + t, rows, :] for t in range(9)]
    km = [w[9 + 8 - t if flip else 18 + t, rows, :] for t in range(9)]
    live = {}
    for r in range(RR):
        lower = [ref[r, 0, rows, :] for ref in (am, a0, ap)]
        upper = [ref[r, 1, rows, :] for ref in (am, a0, ap)]
        both = [u + v for u, v in zip(lower, upper)]
        for q in (1, 0, -1):
            i = r - 1 - q
            if not 0 <= i < NR:
                continue
            total = live.get(i, [None, None, None])
            for s in range(3):
                t = 3 * (q + 1) + s
                terms = (k0[t] * both[s], kp[t] * upper[s], km[t] * lower[s])
                total = [b if a is None else a + b for a, b in zip(total, terms)]
            live[i] = total
        if r >= 2:
            shared, first, second = live.pop(r - 2)
            emit(r - 2, shared + first, shared + second)


def tap_sums_block(g0, a0, am, ap, rows):
    sums = [[None] * 9 for _ in range(3)]
    grads = {}
    for r in range(RR):
        lower = [ref[r, 0, rows, :] for ref in (am, a0, ap)]
        upper = [ref[r, 1, rows, :] for ref in (am, a0, ap)]
        both = [u + v for u, v in zip(lower, upper)]
        if r < NR:
            first = g0[r + 1, 0, rows, :]
            second = g0[r + 1, 1, rows, :]
            grads[r] = (first + second, first, second)
        for q in (1, 0, -1):
            i = r - 1 - q
            if not 0 <= i < NR:
                continue
            shared, first, second = grads[i]
            for s in range(3):
                t = 3 * (q + 1) + s
                terms = (shared * both[s], first * upper[s], second * lower[s])
                for kind in range(3):
                    old = sums[kind][t]
                    sums[kind][t] = terms[kind] if old is None else old + terms[kind]
    lane = iota((BLK, 128), 1)
    out = jnp.zeros((BLK, 128), F32)
    for t in range(9):
        middle = sums[0][t] - sums[1][t] - sums[2][t]
        for p, value in ((0, sums[2][t]), (1, middle), (2, sums[1][t])):
            out = jnp.where(lane == 9 * p + t, jnp.sum(value, axis=1, keepdims=True), out)
    return out


def kernel(
    sizes, factor, phases,
    x_ref, cot_ref, dk_ref, bias_ref, mi_ref, mo_ref,
    ig_ref, kg_ref, mig_ref, bg_ref, mog_ref,
    xf, cf, xb, hb, a0, am, ap, b0, bm, bp, cb, ag, hid, w, mit, mot, turn,
    px, ph, prx, prh, pacc, halo, moa, mia, ba, kc, gs, ar, br, fin, bs,
    hsend, hrecv, asend, arecv, bsend, brecv, csend, crecv,
):
    n_sx, n_sy, n_sample = sizes
    comm = n_sx > 1
    n_group = n_sy * n_sample
    sx, sy, sample = (lax.axis_index(a) for a in ("sx", "sy", "sample"))
    me = sy * n_sample + sample

    def at_group(g):
        return {"sx": sx, "sy": g // n_sample, "sample": g % n_sample}

    def around(dx, dy):
        return {
            "sx": lax.rem(sx + dx + n_sx, n_sx),
            "sy": lax.rem(sy + dy + n_sy, n_sy),
            "sample": sample,
        }

    if comm:
        barrier = pltpu.get_barrier_semaphore()
        for d in range(1, n_group):
            pl.semaphore_signal(barrier, inc=1, device_id=at_group(lax.rem(me + d, n_group)), device_id_type=MESH)
        for d in range(1, n_sx):
            pl.semaphore_signal(barrier, inc=1, device_id=around(d, 0), device_id_type=MESH)
        for dx in (-1, 1):
            for dy in (-1, 1):
                pl.semaphore_signal(barrier, inc=1, device_id=around(dx, dy), device_id_type=MESH)

    pack_to = ((0, 1, 0), (1, 1, 1), (-1, 1, 2), (0, -1, 3), (1, -1, 4), (-1, -1, 5))

    def pack_copy(which, src, dst, slot):
        dx, dy, at = pack_to[slot]
        return pltpu.make_async_remote_copy(
            src_ref=src, dst_ref=dst.at[at], send_sem=hsend.at[which, at], recv_sem=hrecv.at[which, at],
            device_id=around(dx, dy), device_id_type=MESH,
        )

    def slab_copy(which, ref, up):
        return pltpu.make_async_remote_copy(
            src_ref=ref.at[NR if up else 1], dst_ref=ref.at[0 if up else NR + 1],
            send_sem=hsend.at[which, 6 + up], recv_sem=hrecv.at[which, 6 + up],
            device_id=around(1 if up else -1, 0), device_id_type=MESH,
        )

    def rim(recv):
        lane = iota((CH, 128), 1)
        left = lane < 64
        low = jnp.where(left, lane, lane - 64)

        def piece(slot, dx, dy):
            ok = (sx + dx >= 0) & (sx + dx < n_sx) & (sy + dy >= 0) & (sy + dy < n_sy)
            return jnp.where(ok, recv[slot].astype(F32), 0.0)

        mid = jnp.where(left, piece(0, 0, -1), piece(3, 0, 1))
        top = jnp.where(left, piece(1, -1, -1), piece(4, -1, 1))
        end = jnp.where(left, piece(2, 1, -1), piece(5, 1, 1))
        top = pltpu.roll(top, 128 - 16, axis=1)
        end = pltpu.roll(end, 16, axis=1)
        first = (low == 0) | (low == RR)
        last = (low == RR - 1) | (low == 2 * RR - 1)
        return jnp.where(first, top, jnp.where(last, end, mid)).astype(BF16)

    def spread(rows_ref, mid, back, ahead, r, z, edge):
        value = rows_ref[r, z]
        if edge:
            ok = sx > 0 if r == 0 else sx < n_sx - 1
            value = jnp.where(ok, value.astype(F32), 0.0).astype(BF16)
        mid[r, z] = value.astype(F32)
        lhs = jnp.concatenate([value, halo[...]], axis=1)
        rhs = jnp.concatenate([turn[...], rim_matrix(z * RR + r)], axis=0)
        both = dot(lhs, rhs)
        back[r, z] = both[:, :NC]
        ahead[r, z] = both[:, NC:]

    def spread_all(which, rows_ref, mid, back, ahead, sent, recv):
        if comm:
            for slot in range(6):
                pack_copy(which, sent, recv, slot).wait_recv()
            halo[...] = rim(recv)
        else:
            halo[...] = jnp.zeros_like(halo)

        @pl.loop(1, NR + 1)
        def _(r):
            for z in range(2):
                spread(rows_ref, mid, back, ahead, r, z, False)

        if comm:
            slab_copy(which, rows_ref, 0).wait_recv()
            slab_copy(which, rows_ref, 1).wait_recv()
        else:
            rows_ref[0] = jnp.zeros_like(rows_ref[0])
            rows_ref[NR + 1] = jnp.zeros_like(rows_ref[0])
        for r in (0, NR + 1):
            for z in range(2):
                spread(rows_ref, mid, back, ahead, r, z, True)
        if comm:
            for slot in range(6):
                pack_copy(which, sent, recv, slot).wait_send()
            slab_copy(which, rows_ref, 0).wait_send()
            slab_copy(which, rows_ref, 1).wait_send()

    @pl.loop(0, 24)
    def _(k):
        at = pl.ds(pl.multiple_of(k * 256, 256), 256)
        xf[at, :] = x_ref[at, :].astype(F32)

    pacc[...] = jnp.zeros_like(pacc)

    @pl.loop(0, NR)
    def _(i):
        for z in range(2):
            xb[i + 1, z] = xf[pl.ds(z * NR + i, CH, stride=2 * NR), :].astype(BF16)
        pacc[...] += dot(jnp.concatenate([xb[i + 1, 0], xb[i + 1, 1]], axis=1), pack_matrix(i))

    px[...] = pacc[...].astype(BF16)
    if comm:
        pl.semaphore_wait(barrier, n_group - 1 + n_sx - 1 + 4)
        for slot in range(6):
            pack_copy(0, px, prx, slot).start()
        slab_copy(0, xb, 0).start()
        slab_copy(0, xb, 1).start()

    turn[...] = shift_matrix()
    eye = one_hot(iota((CH, CH), 0) == iota((CH, CH), 1))
    mit[...] = dot_nt(eye, mi_ref[...]).astype(BF16)
    mot[...] = dot_nt(eye, mo_ref[...]).astype(BF16)
    tall = jnp.concatenate([dk_ref[...], bias_ref[...], jnp.zeros((100, CH), F32)], axis=0)
    tall = jnp.concatenate([tall, jnp.zeros((128, 64), F32)], axis=1)
    kc[...] = tall.T[:CH]

    @pl.loop(0, CH // BLK)
    def _(b):
        rows = pl.ds(pl.multiple_of(b * BLK, BLK), BLK)
        value = kc[rows, :]
        wide = [jnp.broadcast_to(value[:, k : k + 1], (BLK, 128)) for k in range(28)]
        for t in range(9):
            w[t, rows, :] = wide[9 + t]
            w[9 + t, rows, :] = wide[18 + t] - wide[9 + t]
            w[18 + t, rows, :] = wide[t] - wide[9 + t]
        w[27, rows, :] = wide[27]

    @pl.loop(0, 24)
    def _(k):
        at = pl.ds(pl.multiple_of(k * 256, 256), 256)
        cf[at, :] = cot_ref[at, :].astype(F32)

    @pl.loop(0, NR)
    def _(i):
        value = jnp.concatenate([cf[pl.ds(z * NR + i, CH, stride=2 * NR), :] for z in range(2)], axis=1).astype(BF16)
        cb[i] = value
        ag[i] = dot(mot[...], value)

    spread_all(0, xb, a0, am, ap, px, prx)

    if phases >= 1:
        @pl.loop(0, CH // BLK)
        def _(b):
            rows = pl.ds(pl.multiple_of(b * BLK, BLK), BLK)

            def emit(i, first, second):
                hid[i, rows, 0:NC] = first
                hid[i, rows, NC : 2 * NC] = second

            stencil_block(a0, am, ap, w, False, rows, emit)

    pacc[...] = jnp.zeros_like(pacc)
    moa[...] = jnp.zeros_like(moa)
    mia[...] = jnp.zeros_like(mia)
    ba[...] = jnp.zeros_like(ba)

    if phases >= 2:
        @pl.loop(0, NR)
        def _(i):
            hidden = hid[i].astype(BF16)
            shift = w[27]
            pre = dot(mi_ref[...], hidden) + jnp.concatenate([shift, shift], axis=1)
            cdf = 0.5 * (1.0 + lax.erf(pre * INV_SQRT2))
            dens = jnp.exp(-0.5 * pre * pre) * INV_SQRT2PI
            act = (pre * cdf).astype(BF16)
            pg = (ag[i] * (cdf + pre * dens)).astype(BF16)
            moa[...] += dot_nt(cb[i], act)
            mia[...] += dot_nt(pg, hidden)
            ba[...] += dot_nt(jnp.ones((8, 2 * NC), BF16), pg)
            hg = dot(mit[...], pg).astype(BF16)
            hb[i + 1, 0] = hg[:, :NC]
            hb[i + 1, 1] = hg[:, NC:]
            b0[i + 1, 0] = hg[:, :NC].astype(F32)
            b0[i + 1, 1] = hg[:, NC:].astype(F32)
            pacc[...] += dot(hg, pack_matrix(i))

    ph[...] = pacc[...].astype(BF16)
    if comm:
        for slot in range(6):
            pack_copy(1, ph, prh, slot).start()
        slab_copy(1, hb, 0).start()
        slab_copy(1, hb, 1).start()

    def scatter(g):
        return pltpu.make_async_remote_copy(
            src_ref=gs.at[g], dst_ref=ar.at[me], send_sem=asend.at[g], recv_sem=arecv.at[me],
            device_id=at_group(g), device_id_type=MESH,
        )

    for rg in range(4):
        at = pl.ds(rg * CHUNK, CHUNK)
        gs[rg] = moa[at, 0:128]
        gs[4 + rg] = jnp.concatenate([moa[at, 128:192], mia[at, 0:64]], axis=1)
        gs[8 + rg] = mia[at, 64:192]
    if comm:
        for d in range(1, n_group):
            g = lax.rem(me + d, n_group)

            @pl.when(g < 12)
            def _():
                scatter(g).start()

    if phases >= 3:
        @pl.loop(0, CH // BLK)
        def _(b):
            rows = pl.ds(pl.multiple_of(b * BLK, BLK), BLK)
            kc[rows, :] = tap_sums_block(b0, a0, am, ap, rows)

    flat = jnp.concatenate([kc[...], jnp.zeros((64, 128), F32)], axis=0).T[:32]
    whole = jnp.concatenate([ba[0:1], jnp.zeros((1, 64), F32)], axis=1)
    flat = jnp.where(iota((32, 256), 0) == 27, whole, flat)
    for g in (12, 13):
        gs[g, 0:32] = flat[:, 128 * (g - 12) : 128 * (g - 11)]
        gs[g, 32:48] = jnp.zeros((16, 128), F32)
    for g in (14, 15):
        gs[g] = jnp.zeros((CHUNK, 128), F32)
    if comm:
        for d in range(1, n_group):
            g = lax.rem(me + d, n_group)

            @pl.when(g >= 12)
            def _():
                scatter(g).start()

    spread_all(1, hb, b0, bm, bp, ph, prh)

    def input_grad(start, stop):
        @pl.loop(start, stop)
        def _(b):
            rows = pl.ds(pl.multiple_of(b * BLK, BLK), BLK)

            def emit(i, first, second):
                for z, value in ((0, first), (1, second)):
                    at = pl.ds(b * (BLK * 2 * NR) + z * NR + i, BLK, stride=2 * NR)
                    xf[at, :] = cf[at, :] + value

            stencil_block(b0, bm, bp, w, True, rows, emit)
            at = pl.ds(pl.multiple_of(b * 256, 256), 256)
            ig_ref[at, :] = xf[at, :].astype(BF16)

    def share(d):
        return pltpu.make_async_remote_copy(
            src_ref=bs, dst_ref=br.at[sx], send_sem=bsend.at[d], recv_sem=brecv.at[sx],
            device_id=around(d, 0), device_id_type=MESH,
        )

    def publish(g):
        return pltpu.make_async_remote_copy(
            src_ref=fin.at[me], dst_ref=fin.at[me], send_sem=csend.at[g], recv_sem=crecv.at[me],
            device_id=at_group(g), device_id_type=MESH,
        )

    def arrived(ref, sem, slot):
        pltpu.make_async_remote_copy(
            src_ref=ref.at[slot], dst_ref=ref.at[slot], send_sem=asend.at[0], recv_sem=sem.at[slot],
            device_id=around(1, 0), device_id_type=MESH,
        ).wait_recv()

    if phases >= 4:
        input_grad(0, 8)
    if comm:
        for d in range(1, n_group):
            arrived(ar, arecv, lax.rem(me + d, n_group))
        ar[me] = gs[me]
        total = ar[0]
        for g in range(1, n_group):
            total = total + ar[g]
        bs[...] = total
        for d in range(1, n_sx):
            share(d).start()
        br[sx] = total
    if phases >= 4:
        input_grad(8, 16)
    if comm:
        for d in range(1, n_sx):
            arrived(br, brecv, lax.rem(sx + d, n_sx))
        total = br[0]
        for k in range(1, n_sx):
            total = total + br[k]
        fin[me] = total * factor
        for d in range(1, n_group):
            publish(lax.rem(me + d, n_group)).start()
    if phases >= 4:
        input_grad(16, 24)
    if comm:
        for d in range(1, n_group):
            arrived(fin, crecv, lax.rem(me + d, n_group))
        for d in range(1, n_group):
            g = lax.rem(me + d, n_group)
            scatter(g).wait_send()
            publish(g).wait_send()
        for d in range(1, n_sx):
            share(d).wait_send()
    else:
        fin[...] = gs[...]

    for rg in range(4):
        at = pl.ds(rg * CHUNK, CHUNK)
        mog_ref[at, 0:128] = fin[rg]
        mog_ref[at, 128:192] = fin[4 + rg][:, 0:64]
        mig_ref[at, 0:64] = fin[4 + rg][:, 64:128]
        mig_ref[at, 64:192] = fin[8 + rg]
    kg_ref[:, 0:128] = fin[12][0:27]
    kg_ref[:, 128:192] = fin[13][0:27, 0:64]
    bg_ref[:, 0:128] = fin[12][27:28]
    bg_ref[:, 128:192] = fin[13][27:28, 0:64]


def per_device(sizes, factor, phases, inputs, cotangent, depth_kernel, mix_in, mix_bias, mix_out):
    flat = (CH * 2 * NR, NC)
    vm = pltpu.VMEM
    field = (RR, 2, CH, NC)
    dma = pltpu.SemaphoreType.DMA
    n_sx, n_sy, n_sample = sizes
    n_group = n_sy * n_sample
    scratch = [
        vm(flat, F32), vm(flat, F32),
        vm(field, BF16), vm(field, BF16),
        vm(field, F32), vm(field, F32), vm(field, F32),
        vm(field, F32), vm(field, F32), vm(field, F32),
        vm((NR, CH, 2 * NC), BF16), vm((NR, CH, 2 * NC), F32), vm((NR, CH, 2 * NC), F32),
        vm((28, CH, 128), F32),
        vm((CH, CH), BF16), vm((CH, CH), BF16), vm((NC, 2 * NC), BF16),
        vm((CH, 128), BF16), vm((CH, 128), BF16), vm((6, CH, 128), BF16), vm((6, CH, 128), BF16),
        vm((CH, 128), F32), vm((CH, 128), BF16),
        vm((CH, CH), F32), vm((CH, CH), F32), vm((8, CH), F32), vm((CH, 128), F32),
        vm((16, CHUNK, 128), F32), vm((16, CHUNK, 128), F32), vm((max(n_sx, 2), CHUNK, 128), F32),
        vm((16, CHUNK, 128), F32), vm((CHUNK, 128), F32),
        dma((2, 8)), dma((2, 8)), dma((16,)), dma((16,)), dma((8,)), dma((8,)), dma((16,)), dma((16,)),
    ]
    full = pl.BlockSpec(memory_space=pltpu.VMEM)
    params = dict(vmem_limit_bytes=63 * 1024 * 1024)
    if n_sx > 1:
        params.update(collective_id=0, has_side_effects=True)
    ig, kg, mig, bg, mog = pl.pallas_call(
        functools.partial(kernel, sizes, factor, phases),
        out_shape=(
            jax.ShapeDtypeStruct(flat, BF16),
            jax.ShapeDtypeStruct((27, CH), F32),
            jax.ShapeDtypeStruct((CH, CH), F32),
            jax.ShapeDtypeStruct((1, CH), F32),
            jax.ShapeDtypeStruct((CH, CH), F32),
        ),
        in_specs=[full] * 6,
        out_specs=(full,) * 5,
        scratch_shapes=scratch,
        compiler_params=pltpu.CompilerParams(**params),
        name="block",
    )(
        inputs.reshape(flat),
        cotangent.reshape(flat),
        depth_kernel.T,
        mix_bias.reshape(1, CH),
        mix_in,
        mix_out,
    )
    return (ig.reshape(inputs.shape), kg.T, mig, bg.reshape(CH), mog)


def solution(mesh, phases=9):
    sizes = tuple(mesh.shape[a] for a in ("sx", "sy", "sample"))
    cells = sizes[0] * sizes[1] * sizes[2] * 2 * NR * NC
    field = P("sample", None, None, "sx", "sy")
    return jax.shard_map(
        functools.partial(per_device, sizes, 1.0 / math.sqrt(cells), phases),
        mesh=mesh,
        in_specs=(field, field, P(), P(), P(), P()),
        out_specs=(field, P(), P(), P(), P()),
        check_vma=False,
    )
```

```python
import functools
import math

import jax
import jax.numpy as jnp
from jax import lax
from jax.experimental import pallas as pl
from jax.experimental.pallas import tpu as pltpu
from jax.sharding import PartitionSpec as P

INV_SQRT2 = 0.7071067811865476
INV_SQRT2PI = 0.3989422804014327
MESH = pl.DeviceIdType.MESH
F32 = jnp.float32
BF16 = jnp.bfloat16

CH = 192
NR = 16
NC = 128
RR = NR + 2
BLK = 8
WIDE = 16
CHUNK = 48
MIXES = 12
CHUNKS = 14


def dot(a, b):
    return jnp.dot(a, b, preferred_element_type=F32)


def dot_nt(a, b):
    return lax.dot_general(a, b, (((1,), (1,)), ((), ())), preferred_element_type=F32)


def iota(shape, dim):
    return lax.broadcasted_iota(jnp.int32, shape, dim)


def one_hot(cond):
    return jnp.where(cond, 1.0, 0.0).astype(BF16)


def block_of(b, size):
    return pl.ds(pl.multiple_of(b * size, size), size)


def rim_place(r, z):
    if isinstance(r, int) and r == 0:
        return 64 + 2 * z
    if isinstance(r, int) and r == RR - 1:
        return 68 + 2 * z
    return 4 * (r - 1) + 2 * z


def pick_matrix():
    u = iota((8, 4 * NC), 0)
    k = iota((8, 4 * NC), 1)
    return one_hot(k == (u // 2) * NC + jnp.where(u % 2 == 0, NC - 1, 0))


def rim_matrix(at):
    lane = iota((128, 2 * NC), 0)
    j = iota((128, 2 * NC), 1)
    return one_hot(((j == 0) & (lane == at)) | ((j == 2 * NC - 1) & (lane == at + 1)))


def shift_matrix():
    k = iota((NC, 2 * NC), 0)
    j = iota((NC, 2 * NC), 1)
    return one_hot(((j < NC) & (k == j - 1)) | ((j >= NC) & (k == j - NC + 1)))


def swap_matrix():
    k = iota((256, 256), 0)
    j = iota((256, 256), 1)
    return one_hot((k // 16 == j % 16) & (k % 16 == j // 16))


def tap_matrix(d):
    row = iota((128, 256), 0)
    k = jnp.where(row < 96, row % 32, -2)
    t = 2 * d + jnp.where(iota((128, 256), 1) < 128, 0, 1)
    plus = jnp.where(t < 9, t + 9, jnp.where(t < 18, t + 9, jnp.where(t < 27, t - 18, 27)))
    minus = jnp.where((t < 9) | (t > 26), -1, jnp.where(t < 18, t, t - 9))
    return (jnp.where(k == plus, 1.0, 0.0) - jnp.where(k == minus, 1.0, 0.0)).astype(BF16)


def stencil_block(a0, am, ap, w, flip, rows, emit):
    k0 = [w[8 - t if flip else t, rows, :] for t in range(9)]
    kp = [w[18 + 8 - t if flip else 9 + t, rows, :] for t in range(9)]
    km = [w[9 + 8 - t if flip else 18 + t, rows, :] for t in range(9)]
    live = {}
    for r in range(RR):
        lower = [ref[r, 0, rows, :] for ref in (am, a0, ap)]
        upper = [ref[r, 1, rows, :] for ref in (am, a0, ap)]
        both = [u + v for u, v in zip(lower, upper)]
        for q in (1, 0, -1):
            i = r - 1 - q
            if not 0 <= i < NR:
                continue
            total = live.get(i, [None, None, None])
            for s in range(3):
                t = 3 * (q + 1) + s
                terms = (k0[t] * both[s], kp[t] * upper[s], km[t] * lower[s])
                total = [b if a is None else a + b for a, b in zip(total, terms)]
            live[i] = total
        if r >= 2:
            shared, first, second = live.pop(r - 2)
            emit(r - 2, shared + first, shared + second)


def tap_sums_block(g0, a0, am, ap, rows):
    def step(r, sums):
        sums = list(sums)
        first = g0[r + 1, 0, rows, :]
        second = g0[r + 1, 1, rows, :]
        shared = first + second
        for q in range(3):
            for s, ref in enumerate((am, a0, ap)):
                lower = ref[r + q, 0, rows, :]
                upper = ref[r + q, 1, rows, :]
                t = 3 * q + s
                sums[t] = sums[t] + shared * (lower + upper)
                sums[9 + t] = sums[9 + t] + first * upper
                sums[18 + t] = sums[18 + t] + second * lower
        return tuple(sums)

    sums = lax.fori_loop(0, NR, step, tuple(jnp.zeros((BLK, NC), F32) for _ in range(27)), unroll=8)
    middle = [sums[t] - sums[9 + t] - sums[18 + t] for t in range(9)]
    return list(sums[18:]) + middle + list(sums[9:18])


def kernel(
    sizes, factor,
    x_hbm, cot_hbm, dk_hbm, bias_hbm, mi_hbm, mo_hbm,
    ig_hbm, sums_ref,
    xv, cv, ov, dk, bias, mi, mo,
    xb, hb, a0, am, ap, b0, bm, bp, cb, ag, hid, w, acc, mit, mot, turn, swap,
    px, ph, prx, prh, edge, halo, moa, mia, tall, flat, gs, ar, br, fin, bs,
    load, save, hsend, hrecv, asend, arecv, bsend, brecv, csend, crecv,
):
    n_sx, n_sy, n_sample = sizes
    comm = n_sx > 1
    n_group = n_sy * n_sample
    sx, sy, sample = (lax.axis_index(a) for a in ("sx", "sy", "sample"))
    me = sy * n_sample + sample

    def at_group(g):
        return {"sx": sx, "sy": g // n_sample, "sample": g % n_sample}

    def around(dx, dy):
        return {
            "sx": lax.rem(sx + dx + n_sx, n_sx),
            "sy": lax.rem(sy + dy + n_sy, n_sy),
            "sample": sample,
        }

    third = CH // 3
    loads = [pltpu.make_async_copy(x_hbm.at[pl.ds(third * k, third)], xv.at[pl.ds(third * k, third)], load.at[k]) for k in range(3)]
    loads += [
        pltpu.make_async_copy(src, dst, load.at[3 + k])
        for k, (src, dst) in enumerate(((mi_hbm, mi), (mo_hbm, mo), (dk_hbm, dk), (bias_hbm, bias), (cot_hbm, cv)))
    ]
    with jax.named_scope("start"):
        for copy in loads:
            copy.start()
        if comm:
            barrier = pltpu.get_barrier_semaphore()
            for d in range(1, n_group):
                pl.semaphore_signal(barrier, inc=1, device_id=at_group(lax.rem(me + d, n_group)), device_id_type=MESH)
            for d in range(1, n_sx):
                pl.semaphore_signal(barrier, inc=1, device_id=around(d, 0), device_id_type=MESH)
            for dx in (-1, 1):
                for dy in (-1, 1):
                    pl.semaphore_signal(barrier, inc=1, device_id=around(dx, dy), device_id_type=MESH)

    pack_to = ((0, 1, 0), (1, 1, 1), (-1, 1, 2), (0, -1, 3), (1, -1, 4), (-1, -1, 5))

    def pack_copy(which, src, dst, slot):
        dx, dy, at = pack_to[slot]
        if dx:
            src, dst = src.at[3 if dx > 0 else 0], dst.at[at, 0]
        else:
            dst = dst.at[at]
        return pltpu.make_async_remote_copy(
            src_ref=src, dst_ref=dst, send_sem=hsend.at[which, at], recv_sem=hrecv.at[which, at],
            device_id=around(dx, dy), device_id_type=MESH,
        )

    def slab_copy(which, ref, up):
        return pltpu.make_async_remote_copy(
            src_ref=ref.at[NR if up else 1], dst_ref=ref.at[0 if up else NR + 1],
            send_sem=hsend.at[which, 6 + up], recv_sem=hrecv.at[which, 6 + up],
            device_id=around(1 if up else -1, 0), device_id_type=MESH,
        )

    def pack_edges(sent):
        for k in range(4):
            sent[k] = jnp.concatenate([edge[2 * k], edge[2 * k + 1]], axis=0).astype(BF16)

    def send_edges(which, sent, recv):
        if comm:
            for slot in range(6):
                pack_copy(which, sent, recv, slot).start()

    def rim(recv):
        def piece(slot, block, dx, dy):
            ok = (sx + dx >= 0) & (sx + dx < n_sx) & (sy + dy >= 0) & (sy + dy < n_sy)
            return jnp.where(ok, recv[slot, block].astype(F32), 0.0)

        row = iota((16, CH), 0)
        left = row % 2 == 0
        tall = [jnp.where(left, piece(0, k, 0, -1), piece(3, k, 0, 1)) for k in range(4)]
        top = jnp.where(left, piece(1, 0, -1, -1), piece(4, 0, -1, 1))[8:16]
        end = jnp.where(left, piece(2, 0, 1, -1), piece(5, 0, 1, 1))[0:8]
        tall.append(pltpu.roll(jnp.where(row[0:8] >= 4, top, end), 4, axis=0))
        tall.append(jnp.zeros((128 - 72, CH), F32))
        square = jnp.concatenate(tall, axis=0)
        square = jnp.concatenate([square, jnp.zeros((128, 64), F32)], axis=1)
        return square.T[:CH].astype(BF16)

    def spread(rows_ref, mid, back, ahead, r, z):
        value = rows_ref[r, z]
        if isinstance(r, int):
            ok = sx > 0 if r == 0 else sx < n_sx - 1
            value = jnp.where(ok, value.astype(F32), 0.0).astype(BF16)
        mid[r, z] = value.astype(F32)
        lhs = jnp.concatenate([value, halo[...]], axis=1)
        rhs = jnp.concatenate([turn[...], rim_matrix(rim_place(r, z))], axis=0)
        both = dot(lhs, rhs)
        back[r, z] = both[:, :NC]
        ahead[r, z] = both[:, NC:]

    def spread_all(which, rows_ref, mid, back, ahead, sent, recv):
        if comm:
            for slot in range(6):
                pack_copy(which, sent, recv, slot).wait_recv()
            halo[...] = rim(recv)
        else:
            halo[...] = jnp.zeros_like(halo)

        @pl.loop(1, NR + 1, unroll=4)
        def _(r):
            for z in range(2):
                spread(rows_ref, mid, back, ahead, r, z)

        if comm:
            slab_copy(which, rows_ref, 0).wait_recv()
            slab_copy(which, rows_ref, 1).wait_recv()
        else:
            rows_ref[0] = jnp.zeros_like(rows_ref[0])
            rows_ref[NR + 1] = jnp.zeros_like(rows_ref[0])
        for r in (0, NR + 1):
            for z in range(2):
                spread(rows_ref, mid, back, ahead, r, z)

    with jax.named_scope("rows of x"):
        swap[...] = swap_matrix()
        for k in range(3):
            loads[k].wait()

            @pl.loop(4 * k, 4 * k + 4, unroll=4)
            def _(b):
                part = xv[block_of(b, WIDE)]
                rhs = jnp.concatenate([part[:, z].reshape(WIDE * NR, NC) for z in range(2)], axis=1)
                both = dot(swap[...], rhs).astype(BF16)
                for i in range(NR):
                    for z in range(2):
                        xb[i + 1, z, block_of(b, WIDE), :] = both[WIDE * i : WIDE * (i + 1), NC * z : NC * (z + 1)]

    with jax.named_scope("send x"):
        pick = pick_matrix()
        for i in range(NR // 2):
            four = jnp.concatenate([xb[2 * i + 1 + k // 2, k % 2] for k in range(4)], axis=1)
            edge[i] = dot_nt(pick, four)
        pack_edges(px)
        if comm:
            pl.semaphore_wait(barrier, n_group - 1 + n_sx - 1 + 4)
            slab_copy(0, xb, 0).start()
            slab_copy(0, xb, 1).start()
        send_edges(0, px, prx)

    with jax.named_scope("constants"):
        for k in range(3, 7):
            loads[k].wait()
        turn[...] = shift_matrix()
        eye = one_hot(iota((CH, CH), 0) == iota((CH, CH), 1))
        mit[...] = dot_nt(eye, mi[...]).astype(BF16)
        mot[...] = dot_nt(eye, mo[...]).astype(BF16)

    with jax.named_scope("weights"):
        value = jnp.concatenate([dk[...], bias[...], jnp.zeros((100, CH), F32)], axis=0)
        value = jnp.concatenate([value, jnp.zeros((128, 64), F32)], axis=1).T[:CH]
        high = value.astype(BF16).astype(F32)
        middle = (value - high).astype(BF16).astype(F32)
        low = value - high - middle
        tall[...] = (high + pltpu.roll(middle, 32, axis=1) + pltpu.roll(low, 64, axis=1)).astype(BF16)

        @pl.loop(0, 14, unroll=2)
        def _(d):
            both = dot(tall[...], tap_matrix(d))
            w[2 * d] = both[:, :128]
            w[2 * d + 1] = both[:, 128:]

    loads[7].wait()
    with jax.named_scope("cotangent"):
        @pl.loop(0, CH // WIDE, unroll=4)
        def _(b):
            part = cv[block_of(b, WIDE)]
            rhs = jnp.concatenate([part[:, z].reshape(WIDE * NR, NC) for z in range(2)], axis=1)
            both = dot(swap[...], rhs).astype(BF16)
            for i in range(NR):
                cb[i // 2, block_of(b, WIDE), 256 * (i % 2) : 256 * (i % 2) + 256] = both[WIDE * i : WIDE * (i + 1)]

        @pl.loop(0, NR // 2, unroll=4)
        def _(i):
            ag[i] = dot(mot[...], cb[i])

    with jax.named_scope("spread x"):
        spread_all(0, xb, a0, am, ap, px, prx)

    with jax.named_scope("hidden"):
        @pl.loop(0, CH // BLK)
        def _(b):
            rows = block_of(b, BLK)

            def emit(i, first, second):
                at = 256 * (i % 2)
                hid[i // 2, rows, at : at + 128] = first
                hid[i // 2, rows, at + 128 : at + 256] = second

            stencil_block(a0, am, ap, w, False, rows, emit)

    with jax.named_scope("chain"):
        moa[...] = jnp.zeros_like(moa)
        mia[...] = jnp.zeros_like(mia)

        @pl.loop(0, NR // 2, unroll=4)
        def _(i):
            hidden = hid[i].astype(BF16)
            shift = w[27]
            pre = dot(mi[...], hidden) + jnp.concatenate([shift] * 4, axis=1)
            cdf = 0.5 * (1.0 + lax.erf(pre * INV_SQRT2))
            dens = jnp.exp(-0.5 * pre * pre) * INV_SQRT2PI
            act = (pre * cdf).astype(BF16)
            pg = (ag[i] * (cdf + pre * dens)).astype(BF16)
            moa[...] += dot_nt(cb[i], act)
            mia[...] += dot_nt(pg, jnp.concatenate([hidden, jnp.ones((16, 4 * NC), BF16)], axis=0))
            hg = dot(mit[...], pg).astype(BF16)
            for k in range(4):
                piece = hg[:, NC * k : NC * (k + 1)]
                hb[2 * i + 1 + k // 2, k % 2] = piece
                b0[2 * i + 1 + k // 2, k % 2] = piece.astype(F32)
            edge[i] = dot_nt(pick_matrix(), hg)

    with jax.named_scope("send grad"):
        if comm:
            slab_copy(1, hb, 0).start()
            slab_copy(1, hb, 1).start()
        pack_edges(ph)
        send_edges(1, ph, prh)

    def scatter(g):
        return pltpu.make_async_remote_copy(
            src_ref=gs.at[g], dst_ref=ar.at[me], send_sem=asend.at[g], recv_sem=arecv.at[me],
            device_id=at_group(g), device_id_type=MESH,
        )

    def share(d):
        return pltpu.make_async_remote_copy(
            src_ref=bs, dst_ref=br.at[sx], send_sem=bsend.at[d], recv_sem=brecv.at[sx],
            device_id=around(d, 0), device_id_type=MESH,
        )

    def publish(g):
        return pltpu.make_async_remote_copy(
            src_ref=fin.at[me], dst_ref=fin.at[me], send_sem=csend.at[g], recv_sem=crecv.at[me],
            device_id=at_group(g), device_id_type=MESH,
        )

    def arrived(ref, sem, slot):
        pltpu.make_async_remote_copy(
            src_ref=ref.at[slot], dst_ref=ref.at[slot], send_sem=asend.at[0], recv_sem=sem.at[slot],
            device_id=around(1, 0), device_id_type=MESH,
        ).wait_recv()

    def scatter_all(first, last):
        if comm:
            for d in range(1, n_group):
                g = lax.rem(me + d, n_group)

                @pl.when((g >= first) & (g < last))
                def _():
                    scatter(g).start()

    def sum_group(first, last):
        if comm:
            @pl.when((me >= first) & (me < last))
            def _():
                for d in range(1, n_group):
                    arrived(ar, arecv, lax.rem(me + d, n_group))
                ar[me] = gs[me]
                total = ar[0].astype(F32)
                for g in range(1, n_group):
                    total = total + ar[g].astype(F32)
                bs[...] = total.astype(BF16)
                for d in range(1, n_sx):
                    share(d).start()
                br[sx] = total.astype(BF16)

    def sum_rest(first, last):
        if comm:
            @pl.when((me >= first) & (me < last))
            def _():
                for d in range(1, n_sx):
                    arrived(br, brecv, lax.rem(sx + d, n_sx))
                total = br[0].astype(F32)
                for k in range(1, n_sx):
                    total = total + br[k].astype(F32)
                fin[me] = total.astype(BF16)
                for d in range(1, n_group):
                    publish(lax.rem(me + d, n_group)).start()

    with jax.named_scope("scatter mixes"):
        for rg in range(4):
            at = pl.ds(rg * CHUNK, CHUNK)
            gs[rg] = moa[at, 0:128].astype(BF16)
            gs[4 + rg] = jnp.concatenate([moa[at, 128:192], mia[at, 0:64]], axis=1).astype(BF16)
            gs[8 + rg] = mia[at, 64:192].astype(BF16)
        scatter_all(0, MIXES)

    with jax.named_scope("tap sums"):
        @pl.loop(0, CH // BLK)
        def _(b):
            rows = block_of(b, BLK)
            for k, value in enumerate(tap_sums_block(b0, a0, am, ap, rows)):
                acc[k, rows, :] = value

        acc[27] = jnp.where(iota((CH, NC), 1) == 0, mia[:, 192:193], 0.0)

        @pl.loop(0, 28, unroll=4)
        def _(k):
            value = acc[k]
            high = value.astype(BF16)
            low = (value - high.astype(F32)).astype(BF16)
            flat[k] = dot_nt(jnp.ones((8, 2 * NC), BF16), jnp.concatenate([high, low], axis=1))

    with jax.named_scope("scatter taps"):
        value = jnp.concatenate([flat[k, 0:1] for k in range(28)] + [jnp.zeros((20, CH), F32)], axis=0)
        gs[12] = value[:, 0:128].astype(BF16)
        gs[13] = jnp.concatenate([value[:, 128:192], jnp.zeros((CHUNK, 64), F32)], axis=1).astype(BF16)
        scatter_all(MIXES, CHUNKS)

    with jax.named_scope("spread grad"):
        spread_all(1, hb, b0, bm, bp, ph, prh)

    with jax.named_scope("sum mixes"):
        sum_group(0, MIXES)

    def input_grad(part):
        @pl.loop(8 * part, 8 * part + 8)
        def _(b):
            rows = block_of(b, BLK)

            def emit(i, first, second):
                at = 256 * (i % 2)
                ag[i // 2, rows, at : at + 128] = first
                ag[i // 2, rows, at + 128 : at + 256] = second

            stencil_block(b0, bm, bp, w, True, rows, emit)

        @pl.loop(4 * part, 4 * part + 4, unroll=4)
        def _(b):
            rows = block_of(b, WIDE)
            rhs = [ag[i // 2, rows, 256 * (i % 2) : 256 * (i % 2) + 256].astype(BF16) for i in range(NR)]
            both = dot(swap[...], jnp.concatenate(rhs, axis=0))
            for z in range(2):
                value = both[:, NC * z : NC * (z + 1)].reshape(WIDE, NR, NC)
                ov[rows, z] = (cv[rows, z].astype(F32) + value).astype(BF16)

    def save_part(part):
        at = pl.ds(third * part, third)
        return pltpu.make_async_copy(ov.at[at], ig_hbm.at[at], save.at[part])

    with jax.named_scope("grad 1"):
        input_grad(0)
    save_part(0).start()
    with jax.named_scope("sum taps"):
        sum_group(MIXES, CHUNKS)
        sum_rest(0, MIXES)
    with jax.named_scope("grad 2"):
        input_grad(1)
    save_part(1).start()
    with jax.named_scope("sum taps 2"):
        sum_rest(MIXES, CHUNKS)
    with jax.named_scope("grad 3"):
        input_grad(2)
    save_part(2).start()

    with jax.named_scope("finish"):
        if comm:
            for which, rows_ref, sent, recv in ((0, xb, px, prx), (1, hb, ph, prh)):
                for slot in range(6):
                    pack_copy(which, sent, recv, slot).wait_send()
                slab_copy(which, rows_ref, 0).wait_send()
                slab_copy(which, rows_ref, 1).wait_send()
            for g in range(CHUNKS):
                @pl.when(me != g)
                def _():
                    scatter(g).wait_send()
                    arrived(fin, crecv, g)

            @pl.when(me < CHUNKS)
            def _():
                for d in range(1, n_sx):
                    share(d).wait_send()
                for d in range(1, n_group):
                    publish(lax.rem(me + d, n_group)).wait_send()
        else:
            fin[...] = gs[...]
        sums_ref[...] = fin[...].astype(F32) * factor
        for part in range(3):
            save_part(part).wait()


def deliver(ig_in, sums_ref, ig_out, kg_ref, mig_ref, bg_ref, mog_ref, held, sems):
    parts = ig_in.shape[0] // 4
    at = [pl.ds(parts * k, parts) for k in range(4)]
    inward = [pltpu.make_async_copy(ig_in.at[at[k]], held.at[at[k]], sems.at[0, k]) for k in range(4)]
    outward = [pltpu.make_async_copy(held.at[at[k]], ig_out.at[at[k]], sems.at[1, k]) for k in range(4)]
    for copy in inward:
        copy.start()
    for rg in range(4):
        rows = pl.ds(rg * CHUNK, CHUNK)
        mog_ref[rows, 0:128] = sums_ref[rg]
        mog_ref[rows, 128:192] = sums_ref[4 + rg, :, 0:64]
        mig_ref[rows, 0:64] = sums_ref[4 + rg, :, 64:128]
        mig_ref[rows, 64:192] = sums_ref[8 + rg]
    kg_ref[:, 0:128] = sums_ref[12, 0:27]
    kg_ref[:, 128:192] = sums_ref[13, 0:27, 0:64]
    bg_ref[:, 0:128] = sums_ref[12, 27:28]
    bg_ref[:, 128:192] = sums_ref[13, 27:28, 0:64]
    for first, second in zip(inward, outward):
        first.wait()
        second.start()
    for copy in outward:
        copy.wait()


def per_device(sizes, factor, inputs, cotangent, depth_kernel, mix_in, mix_bias, mix_out):
    tile = (CH, 2, NR, NC)
    vm = pltpu.VMEM
    field = (RR, 2, CH, NC)
    pairs = (NR // 2, CH, 4 * NC)
    dma = pltpu.SemaphoreType.DMA
    n_sx, n_sy, n_sample = sizes
    sums = (CHUNKS, CHUNK, 128)
    scratch = [
        vm(tile, BF16), vm(tile, BF16), vm(tile, BF16),
        vm((27, CH), F32), vm((1, CH), F32), vm((CH, CH), BF16), vm((CH, CH), BF16),
        vm(field, BF16), vm(field, BF16),
        vm(field, F32), vm(field, F32), vm(field, F32),
        vm(field, F32), vm(field, F32), vm(field, F32),
        vm(pairs, BF16), vm(pairs, F32), vm(pairs, F32),
        vm((28, CH, 128), F32), vm((28, CH, 128), F32),
        vm((CH, CH), BF16), vm((CH, CH), BF16), vm((NC, 2 * NC), BF16), vm((256, 256), BF16),
        vm((4, 16, CH), BF16), vm((4, 16, CH), BF16), vm((6, 4, 16, CH), BF16), vm((6, 4, 16, CH), BF16),
        vm((NR // 2, 8, CH), F32), vm((CH, 128), BF16),
        vm((CH, CH), F32), vm((CH, CH + 16), F32), vm((CH, 128), BF16), vm((28, 8, CH), F32),
        vm(sums, BF16), vm((16, CHUNK, 128), BF16), vm((8, CHUNK, 128), BF16),
        vm(sums, BF16), vm((CHUNK, 128), BF16),
        dma((8,)), dma((3,)), dma((2, 8)), dma((2, 8)),
        dma((16,)), dma((16,)), dma((8,)), dma((8,)), dma((16,)), dma((16,)),
    ]
    here = pl.BlockSpec(memory_space=pltpu.VMEM)
    there = pl.BlockSpec(memory_space=pl.ANY)
    params = dict(vmem_limit_bytes=60 * 1024 * 1024)
    if n_sx > 1:
        params.update(collective_id=0, has_side_effects=True)
    ig, sums = pl.pallas_call(
        functools.partial(kernel, sizes, factor),
        out_shape=(jax.ShapeDtypeStruct(tile, BF16), jax.ShapeDtypeStruct(sums, F32)),
        in_specs=[there] * 6,
        out_specs=(there, here),
        scratch_shapes=scratch,
        compiler_params=pltpu.CompilerParams(**params),
        name="block",
    )(
        inputs.reshape(tile),
        cotangent.reshape(tile),
        depth_kernel.T,
        mix_bias.reshape(1, CH),
        mix_in,
        mix_out,
    )
    ig, kg, mig, bg, mog = pl.pallas_call(
        deliver,
        out_shape=(
            jax.ShapeDtypeStruct(tile, BF16),
            jax.ShapeDtypeStruct((27, CH), F32),
            jax.ShapeDtypeStruct((CH, CH), F32),
            jax.ShapeDtypeStruct((1, CH), F32),
            jax.ShapeDtypeStruct((CH, CH), F32),
        ),
        in_specs=[there, here],
        out_specs=(there, here, here, here, here),
        scratch_shapes=[vm(tile, BF16), dma((2, 4))],
        name="deliver",
    )(ig, sums)
    return (ig.reshape(inputs.shape), kg.T, mig, bg.reshape(CH), mog)


def solution(mesh):
    sizes = tuple(mesh.shape[a] for a in ("sx", "sy", "sample"))
    cells = sizes[0] * sizes[1] * sizes[2] * 2 * NR * NC
    field = P("sample", None, None, "sx", "sy")
    return jax.shard_map(
        functools.partial(per_device, sizes, 1.0 / math.sqrt(cells)),
        mesh=mesh,
        in_specs=(field, field, P(), P(), P(), P()),
        out_specs=(field, P(), P(), P(), P()),
        check_vma=False,
    )
```

```python
import functools
import math

import jax
import jax.numpy as jnp
from jax import lax
from jax.experimental import pallas as pl
from jax.experimental.pallas import tpu as pltpu
from jax.sharding import PartitionSpec as P

INV_SQRT2 = 0.7071067811865476
INV_SQRT2PI = 0.3989422804014327
MESH = pl.DeviceIdType.MESH
F32 = jnp.float32
BF16 = jnp.bfloat16

CH = 192
NR = 16
NC = 128
RR = NR + 2
BLK = 8
WIDE = 16
CHUNK = 48
PIECE = 80
PARTS = 8


def dot(a, b):
    return jnp.dot(a, b, preferred_element_type=F32)


def dot_nt(a, b):
    return lax.dot_general(a, b, (((1,), (1,)), ((), ())), preferred_element_type=F32)


def iota(shape, dim):
    return lax.broadcasted_iota(jnp.int32, shape, dim)


def one_hot(cond):
    return jnp.where(cond, 1.0, 0.0).astype(BF16)


def block_of(b, size):
    return pl.ds(pl.multiple_of(b * size, size), size)


def rim_place(r, z):
    if isinstance(r, int) and r == 0:
        return 64 + 2 * z
    if isinstance(r, int) and r == RR - 1:
        return 68 + 2 * z
    return 4 * (r - 1) + 2 * z


def pick_matrix():
    u = iota((8, 4 * NC), 0)
    k = iota((8, 4 * NC), 1)
    return one_hot(k == (u // 2) * NC + jnp.where(u % 2 == 0, NC - 1, 0))


def rim_matrix(at):
    lane = iota((128, 2 * NC), 0)
    j = iota((128, 2 * NC), 1)
    return one_hot(((j == 0) & (lane == at)) | ((j == 2 * NC - 1) & (lane == at + 1)))


def shift_matrix():
    k = iota((NC, 2 * NC), 0)
    j = iota((NC, 2 * NC), 1)
    return one_hot(((j < NC) & (k == j - 1)) | ((j >= NC) & (k == j - NC + 1)))


def swap_matrix():
    k = iota((256, 256), 0)
    j = iota((256, 256), 1)
    return one_hot((k // 16 == j % 16) & (k % 16 == j // 16))


def tap_matrix(d):
    row = iota((128, 256), 0)
    k = jnp.where(row < 96, row % 32, -2)
    t = 2 * d + jnp.where(iota((128, 256), 1) < 128, 0, 1)
    plus = jnp.where(t < 9, t + 9, jnp.where(t < 18, t + 9, jnp.where(t < 27, t - 18, 27)))
    minus = jnp.where((t < 9) | (t > 26), -1, jnp.where(t < 18, t, t - 9))
    return (jnp.where(k == plus, 1.0, 0.0) - jnp.where(k == minus, 1.0, 0.0)).astype(BF16)


def stencil_block(a0, am, ap, w, flip, rows, emit):
    k0 = [w[8 - t if flip else t, rows, :] for t in range(9)]
    kp = [w[18 + 8 - t if flip else 9 + t, rows, :] for t in range(9)]
    km = [w[9 + 8 - t if flip else 18 + t, rows, :] for t in range(9)]
    live = {}
    for r in range(RR):
        lower = [ref[r, 0, rows, :] for ref in (am, a0, ap)]
        upper = [ref[r, 1, rows, :] for ref in (am, a0, ap)]
        both = [u + v for u, v in zip(lower, upper)]
        for q in (1, 0, -1):
            i = r - 1 - q
            if not 0 <= i < NR:
                continue
            total = live.get(i, [None, None, None])
            for s in range(3):
                t = 3 * (q + 1) + s
                terms = (k0[t] * both[s], kp[t] * upper[s], km[t] * lower[s])
                total = [b if a is None else a + b for a, b in zip(total, terms)]
            live[i] = total
        if r >= 2:
            shared, first, second = live.pop(r - 2)
            emit(r - 2, shared + first, shared + second)


def tap_sums_block(g0, a0, am, ap, rows):
    def step(r, sums):
        sums = list(sums)
        first = g0[r + 1, 0, rows, :]
        second = g0[r + 1, 1, rows, :]
        shared = first + second
        for q in range(3):
            for s, ref in enumerate((am, a0, ap)):
                lower = ref[r + q, 0, rows, :]
                upper = ref[r + q, 1, rows, :]
                t = 3 * q + s
                sums[t] = sums[t] + shared * (lower + upper)
                sums[9 + t] = sums[9 + t] + first * upper
                sums[18 + t] = sums[18 + t] + second * lower
        return tuple(sums)

    sums = lax.fori_loop(0, NR, step, tuple(jnp.zeros((BLK, NC), F32) for _ in range(27)), unroll=8)
    middle = [sums[t] - sums[9 + t] - sums[18 + t] for t in range(9)]
    return list(sums[18:]) + middle + list(sums[9:18])


def kernel(
    sizes, factor,
    x_hbm, cot_hbm, dk_hbm, bias_hbm, mi_hbm, mo_hbm,
    ig_hbm, sums_hbm,
    xv, cv, ov, sums_ref, dk, bias, mi, mo,
    xb, hb, a0, am, ap, b0, bm, bp, cb, ag, hid, w, acc, mit, mot, turn, swap,
    px, ph, prx, prh, edge, halo, moa, mia, tall, flat, gs, ar, br, fin, bs, pgs, ks, kr, kt, kg,
    load, save, hsend, hrecv, asend, arecv, bsend, brecv, csend, crecv, ksend, krecv, lsend, lrecv,
):
    n_sx, n_sy, n_sample = sizes
    comm = n_sx > 1
    n_group = n_sy * n_sample
    sx, sy, sample = (lax.axis_index(a) for a in ("sx", "sy", "sample"))
    me = sy * n_sample + sample

    def at_group(g):
        return {"sx": sx, "sy": g // n_sample, "sample": g % n_sample}

    def around(dx, dy):
        return {
            "sx": lax.rem(sx + dx + n_sx, n_sx),
            "sy": lax.rem(sy + dy + n_sy, n_sy),
            "sample": sample,
        }

    third = CH // 3
    loads = [pltpu.make_async_copy(x_hbm.at[pl.ds(third * k, third)], xv.at[pl.ds(third * k, third)], load.at[k]) for k in range(3)]
    loads += [
        pltpu.make_async_copy(src, dst, load.at[3 + k])
        for k, (src, dst) in enumerate(((mi_hbm, mi), (mo_hbm, mo), (dk_hbm, dk), (bias_hbm, bias), (cot_hbm, cv)))
    ]
    with jax.named_scope("start"):
        for copy in loads[:7]:
            copy.start()
        if comm:
            barrier = pltpu.get_barrier_semaphore()
            for d in range(1, n_group):
                pl.semaphore_signal(barrier, inc=1, device_id=at_group(lax.rem(me + d, n_group)), device_id_type=MESH)
            for d in range(1, n_sx):
                pl.semaphore_signal(barrier, inc=1, device_id=around(d, 0), device_id_type=MESH)
            for dx in (-1, 1):
                for dy in (-1, 1):
                    pl.semaphore_signal(barrier, inc=1, device_id=around(dx, dy), device_id_type=MESH)

    pack_to = ((0, 1, 0), (1, 1, 1), (-1, 1, 2), (0, -1, 3), (1, -1, 4), (-1, -1, 5))

    def pack_copy(which, src, dst, slot):
        dx, dy, at = pack_to[slot]
        if dx:
            src, dst = src.at[3 if dx > 0 else 0], dst.at[at, 0]
        else:
            dst = dst.at[at]
        return pltpu.make_async_remote_copy(
            src_ref=src, dst_ref=dst, send_sem=hsend.at[which, at], recv_sem=hrecv.at[which, at],
            device_id=around(dx, dy), device_id_type=MESH,
        )

    def slab_copy(which, ref, up, k):
        part = pl.ds(third * k, third)
        return pltpu.make_async_remote_copy(
            src_ref=ref.at[NR if up else 1, :, part], dst_ref=ref.at[0 if up else NR + 1, :, part],
            send_sem=hsend.at[which, 6 + 3 * up + k], recv_sem=hrecv.at[which, 6 + 3 * up + k],
            device_id=around(1 if up else -1, 0), device_id_type=MESH,
        )

    def pack_edges(sent):
        for k in range(4):
            sent[k] = jnp.concatenate([edge[2 * k], edge[2 * k + 1]], axis=0).astype(BF16)

    def send_edges(which, sent, recv):
        if comm:
            for slot in range(6):
                pack_copy(which, sent, recv, slot).start()

    def rim(recv):
        def piece(slot, block, dx, dy):
            ok = (sx + dx >= 0) & (sx + dx < n_sx) & (sy + dy >= 0) & (sy + dy < n_sy)
            return jnp.where(ok, recv[slot, block].astype(F32), 0.0)

        row = iota((16, CH), 0)
        left = row % 2 == 0
        tall = [jnp.where(left, piece(0, k, 0, -1), piece(3, k, 0, 1)) for k in range(4)]
        top = jnp.where(left, piece(1, 0, -1, -1), piece(4, 0, -1, 1))[8:16]
        end = jnp.where(left, piece(2, 0, 1, -1), piece(5, 0, 1, 1))[0:8]
        tall.append(pltpu.roll(jnp.where(row[0:8] >= 4, top, end), 4, axis=0))
        tall.append(jnp.zeros((128 - 72, CH), F32))
        square = jnp.concatenate(tall, axis=0)
        square = jnp.concatenate([square, jnp.zeros((128, 64), F32)], axis=1)
        return square.T[:CH].astype(BF16)

    def spread(rows_ref, mid, back, ahead, r, z):
        value = rows_ref[r, z]
        if isinstance(r, int):
            ok = sx > 0 if r == 0 else sx < n_sx - 1
            value = jnp.where(ok, value.astype(F32), 0.0).astype(BF16)
        mid[r, z] = value.astype(F32)
        lhs = jnp.concatenate([value, halo[...]], axis=1)
        rhs = jnp.concatenate([turn[...], rim_matrix(rim_place(r, z))], axis=0)
        both = dot(lhs, rhs)
        back[r, z] = both[:, :NC]
        ahead[r, z] = both[:, NC:]

    def spread_all(which, rows_ref, mid, back, ahead, sent, recv):
        if comm:
            for slot in range(6):
                pack_copy(which, sent, recv, slot).wait_recv()
            halo[...] = rim(recv)
        else:
            halo[...] = jnp.zeros_like(halo)

        @pl.loop(1, NR + 1, unroll=4)
        def _(r):
            for z in range(2):
                spread(rows_ref, mid, back, ahead, r, z)

        if comm:
            for k in range(3):
                slab_copy(which, rows_ref, 0, k).wait_recv()
                slab_copy(which, rows_ref, 1, k).wait_recv()
        else:
            rows_ref[0] = jnp.zeros_like(rows_ref[0])
            rows_ref[NR + 1] = jnp.zeros_like(rows_ref[0])
        for r in (0, NR + 1):
            for z in range(2):
                spread(rows_ref, mid, back, ahead, r, z)

    with jax.named_scope("rows of x"):
        swap[...] = swap_matrix()
        for k in range(3):
            loads[k].wait()

            @pl.loop(4 * k, 4 * k + 4, unroll=4)
            def _(b):
                part = xv[block_of(b, WIDE)]
                rhs = jnp.concatenate([part[:, z].reshape(WIDE * NR, NC) for z in range(2)], axis=1)
                both = dot(swap[...], rhs).astype(BF16)
                for i in range(NR):
                    for z in range(2):
                        xb[i + 1, z, block_of(b, WIDE), :] = both[WIDE * i : WIDE * (i + 1), NC * z : NC * (z + 1)]

            if comm:
                if k == 0:
                    pl.semaphore_wait(barrier, n_group - 1 + n_sx - 1 + 4)
                slab_copy(0, xb, 0, k).start()
                slab_copy(0, xb, 1, k).start()
        loads[7].start()

    with jax.named_scope("send x"):
        pick = pick_matrix()
        for i in range(NR // 2):
            four = jnp.concatenate([xb[2 * i + 1 + k // 2, k % 2] for k in range(4)], axis=1)
            edge[i] = dot_nt(pick, four)
        pack_edges(px)
        send_edges(0, px, prx)

    with jax.named_scope("constants"):
        for k in range(3, 7):
            loads[k].wait()
        turn[...] = shift_matrix()
        eye = one_hot(iota((CH, CH), 0) == iota((CH, CH), 1))
        mit[...] = dot_nt(eye, mi[...]).astype(BF16)
        mot[...] = dot_nt(eye, mo[...]).astype(BF16)

    with jax.named_scope("weights"):
        value = jnp.concatenate([dk[...], bias[...], jnp.zeros((100, CH), F32)], axis=0)
        value = jnp.concatenate([value, jnp.zeros((128, 64), F32)], axis=1).T[:CH]
        high = value.astype(BF16).astype(F32)
        middle = (value - high).astype(BF16).astype(F32)
        low = value - high - middle
        tall[...] = (high + pltpu.roll(middle, 32, axis=1) + pltpu.roll(low, 64, axis=1)).astype(BF16)

        @pl.loop(0, 14, unroll=7)
        def _(d):
            both = dot(tall[...], tap_matrix(d))
            w[2 * d] = both[:, :128]
            w[2 * d + 1] = both[:, 128:]

    loads[7].wait()
    with jax.named_scope("cotangent"):
        @pl.loop(0, CH // WIDE, unroll=4)
        def _(b):
            part = cv[block_of(b, WIDE)]
            rhs = jnp.concatenate([part[:, z].reshape(WIDE * NR, NC) for z in range(2)], axis=1)
            both = dot(swap[...], rhs).astype(BF16)
            for i in range(NR):
                cb[i // 2, block_of(b, WIDE), 256 * (i % 2) : 256 * (i % 2) + 256] = both[WIDE * i : WIDE * (i + 1)]

        @pl.loop(0, NR // 2, unroll=4)
        def _(i):
            ag[i] = dot(mot[...], cb[i])

    with jax.named_scope("spread x"):
        spread_all(0, xb, a0, am, ap, px, prx)

    with jax.named_scope("hidden"):
        @pl.loop(0, CH // BLK)
        def _(b):
            rows = block_of(b, BLK)

            def emit(i, first, second):
                at = 256 * (i % 2)
                hid[i // 2, rows, at : at + 128] = first
                hid[i // 2, rows, at + 128 : at + 256] = second

            stencil_block(a0, am, ap, w, False, rows, emit)

    with jax.named_scope("chain"):
        moa[...] = jnp.zeros_like(moa)
        mia[...] = jnp.zeros_like(mia)

        @pl.loop(0, NR // 2, unroll=4)
        def _(i):
            hidden = hid[i].astype(BF16)
            shift = w[27]
            pre = dot(mi[...], hidden) + jnp.concatenate([shift] * 4, axis=1)
            cdf = 0.5 * (1.0 + lax.erf(pre * INV_SQRT2))
            dens = jnp.exp(-0.5 * pre * pre) * INV_SQRT2PI
            act = (pre * cdf).astype(BF16)
            pg = (ag[i] * (cdf + pre * dens)).astype(BF16)
            moa[...] += dot_nt(cb[i], act)
            mia[...] += dot_nt(pg, jnp.concatenate([hidden, jnp.ones((16, 4 * NC), BF16)], axis=0))
            pgs[i] = pg

    def over_sx(src, dst, sends, recvs, d):
        return pltpu.make_async_remote_copy(
            src_ref=src, dst_ref=dst.at[sx], send_sem=sends.at[d], recv_sem=recvs.at[sx],
            device_id=around(d, 0), device_id_type=MESH,
        )

    def over_group(src, dst, sends, recvs, d):
        return pltpu.make_async_remote_copy(
            src_ref=src, dst_ref=dst.at[me], send_sem=sends.at[d], recv_sem=recvs.at[me],
            device_id=at_group(lax.rem(me + d, n_group)), device_id_type=MESH,
        )

    def scatter(d):
        return over_sx(gs.at[lax.rem(sx + d, n_sx)], ar, asend, arecv, d)

    def publish(d):
        return over_sx(fin.at[sx], fin, csend, crecv, d)

    def arrived(ref, sem, slot):
        pltpu.make_async_remote_copy(
            src_ref=ref.at[slot], dst_ref=ref.at[slot], send_sem=asend.at[0], recv_sem=sem.at[slot],
            device_id=around(1, 0), device_id_type=MESH,
        ).wait_recv()

    def arrived_sx(ref, sem):
        for d in range(1, n_sx):
            arrived(ref, sem, lax.rem(sx + d, n_sx))

    def arrived_group(ref, sem):
        for d in range(1, n_group):
            arrived(ref, sem, lax.rem(me + d, n_group))

    def added(ref, count):
        total = ref[0].astype(F32)
        for k in range(1, count):
            total = total + ref[k].astype(F32)
        return total

    def sum_sx():
        if comm:
            arrived_sx(ar, arecv)
            ar[sx] = gs[sx]
            bs[...] = added(ar, n_sx).astype(BF16)
            for d in range(1, n_group):
                over_group(bs, br, bsend, brecv, d).start()
            br[me] = bs[...]

    def sum_group():
        if comm:
            arrived_group(br, brecv)
            fin[sx] = added(br, n_group).astype(BF16)
            for d in range(1, n_sx):
                publish(d).start()

    def sum_taps():
        if comm:
            arrived_sx(kr, krecv)
            kr[sx] = ks[...]
            kt[...] = added(kr, n_sx).astype(BF16)
            for d in range(1, n_group):
                over_group(kt, kg, lsend, lrecv, d).start()
            kg[me] = kt[...]

    with jax.named_scope("scatter mixes"):
        for k in range(PARTS):
            at = pl.ds(24 * k, 24)
            mid = jnp.concatenate([moa[at, 128:192], mia[at, 0:64]], axis=1)
            value = jnp.concatenate([moa[at, 0:128], mid, mia[at, 64:192], jnp.zeros((8, 128), F32)], axis=0)
            gs[k] = value.astype(BF16)
        if comm:
            for d in range(1, n_sx):
                scatter(d).start()

    with jax.named_scope("hidden grad"):
        @pl.loop(0, NR // 2, unroll=4)
        def _(i):
            hg = dot(mit[...], pgs[i]).astype(BF16)
            for k in range(4):
                piece = hg[:, NC * k : NC * (k + 1)]
                hb[2 * i + 1 + k // 2, k % 2] = piece
                b0[2 * i + 1 + k // 2, k % 2] = piece.astype(F32)
            edge[i] = dot_nt(pick_matrix(), hg)

    with jax.named_scope("send grad"):
        if comm:
            for k in range(3):
                slab_copy(1, hb, 0, k).start()
                slab_copy(1, hb, 1, k).start()
        pack_edges(ph)
        send_edges(1, ph, prh)

    def tap_sums(start, stop):
        @pl.loop(start, stop)
        def _(b):
            rows = block_of(b, BLK)
            for k, value in enumerate(tap_sums_block(b0, a0, am, ap, rows)):
                acc[k, rows, :] = value

    with jax.named_scope("tap sums"):
        tap_sums(0, 14)
    with jax.named_scope("sum sx"):
        sum_sx()
    with jax.named_scope("tap sums 2"):
        tap_sums(14, 24)
        acc[27] = jnp.where(iota((CH, NC), 1) == 0, mia[:, 192:193], 0.0)

        for k in range(28):
            value = acc[k]
            high = value.astype(BF16)
            low = (value - high.astype(F32)).astype(BF16)
            flat[k] = dot_nt(jnp.ones((8, 2 * NC), BF16), jnp.concatenate([high, low], axis=1))

    with jax.named_scope("scatter taps"):
        value = jnp.concatenate([flat[k, 0:1] for k in range(28)] + [jnp.zeros((4, CH), F32)], axis=0)
        ks[0:32] = value[:, 0:128].astype(BF16)
        ks[32:48] = jnp.concatenate([value[0:16, 128:192], value[16:32, 128:192]], axis=1).astype(BF16)
        if comm:
            for d in range(1, n_sx):
                over_sx(ks, kr, ksend, krecv, d).start()

    with jax.named_scope("spread grad"):
        spread_all(1, hb, b0, bm, bp, ph, prh)

    def input_grad(part):
        @pl.loop(8 * part, 8 * part + 8)
        def _(b):
            rows = block_of(b, BLK)

            def emit(i, first, second):
                at = 256 * (i % 2)
                ag[i // 2, rows, at : at + 128] = first
                ag[i // 2, rows, at + 128 : at + 256] = second

            stencil_block(b0, bm, bp, w, True, rows, emit)

        @pl.loop(4 * part, 4 * part + 4, unroll=4)
        def _(b):
            rows = block_of(b, WIDE)
            rhs = [ag[i // 2, rows, 256 * (i % 2) : 256 * (i % 2) + 256].astype(BF16) for i in range(NR)]
            both = dot(swap[...], jnp.concatenate(rhs, axis=0))
            for z in range(2):
                value = both[:, NC * z : NC * (z + 1)].reshape(WIDE, NR, NC)
                ov[rows, z] = (cv[rows, z].astype(F32) + value).astype(BF16)

    def save_part(part):
        at = pl.ds(third * part, third)
        return pltpu.make_async_copy(ov.at[at], ig_hbm.at[at], save.at[part])

    with jax.named_scope("grad 1"):
        input_grad(0)
    save_part(0).start()
    with jax.named_scope("sum rest"):
        sum_taps()
        sum_group()
    with jax.named_scope("grad 2"):
        input_grad(1)
    save_part(1).start()
    with jax.named_scope("grad 3"):
        input_grad(2)
    save_part(2).start()

    with jax.named_scope("finish"):
        if comm:
            for which, rows_ref, sent, recv in ((0, xb, px, prx), (1, hb, ph, prh)):
                for slot in range(6):
                    pack_copy(which, sent, recv, slot).wait_send()
                for k in range(3):
                    slab_copy(which, rows_ref, 0, k).wait_send()
                    slab_copy(which, rows_ref, 1, k).wait_send()
            for d in range(1, n_sx):
                scatter(d).wait_send()
                over_sx(ks, kr, ksend, krecv, d).wait_send()
                publish(d).wait_send()
            for d in range(1, n_group):
                over_group(bs, br, bsend, brecv, d).wait_send()
                over_group(kt, kg, lsend, lrecv, d).wait_send()
            arrived_sx(fin, crecv)
            arrived_group(kg, lrecv)
            sums_ref[PARTS, 0:CHUNK] = added(kg, n_group) * factor
        else:
            fin[...] = gs[...]
            sums_ref[PARTS, 0:CHUNK] = ks[...].astype(F32) * factor
        sums_ref[PARTS, CHUNK:PIECE] = jnp.zeros((PIECE - CHUNK, 128), F32)
        sums_ref[0:PARTS] = fin[...].astype(F32) * factor
        last = pltpu.make_async_copy(sums_ref, sums_hbm, save.at[3])
        last.start()
        for part in range(3):
            save_part(part).wait()
        last.wait()


def deliver(ig_in, sums_in, ig_out, kg_out, mig_out, bg_out, mog_out, held, sums, kg, mig, bg, mog, sems):
    parts = CH // 4
    at = [pl.ds(parts * k, parts) for k in range(4)]
    inward = [pltpu.make_async_copy(ig_in.at[at[k]], held.at[at[k]], sems.at[0, k]) for k in range(4)]
    outward = [pltpu.make_async_copy(held.at[at[k]], ig_out.at[at[k]], sems.at[1, k]) for k in range(4)]
    first = pltpu.make_async_copy(sums_in, sums, sems.at[0, 4])
    first.start()
    for copy in inward:
        copy.start()
    first.wait()
    for k in range(PARTS):
        rows = pl.ds(24 * k, 24)
        mog[rows, 0:128] = sums[k, 0:24]
        mog[rows, 128:192] = sums[k, 24:48, 0:64]
        mig[rows, 0:64] = sums[k, 24:48, 64:128]
        mig[rows, 64:192] = sums[k, 48:72]
    kg[:, 0:128] = sums[PARTS, 0:27]
    kg[0:16, 128:192] = sums[PARTS, 32:48, 0:64]
    kg[16:27, 128:192] = sums[PARTS, 32:43, 64:128]
    bg[:, 0:128] = sums[PARTS, 27:28]
    bg[:, 128:192] = sums[PARTS, 43:44, 64:128]
    pairs = ((kg, kg_out), (mig, mig_out), (bg, bg_out), (mog, mog_out))
    small = [pltpu.make_async_copy(src, dst, sems.at[1, 4 + k]) for k, (src, dst) in enumerate(pairs)]
    for copy in small:
        copy.start()
    for k in range(4):
        inward[k].wait()
        outward[k].start()
    for copy in outward + small:
        copy.wait()


def per_device(sizes, factor, inputs, cotangent, depth_kernel, mix_in, mix_bias, mix_out):
    tile = (CH, 2, NR, NC)
    vm = pltpu.VMEM
    field = (RR, 2, CH, NC)
    pairs = (NR // 2, CH, 4 * NC)
    dma = pltpu.SemaphoreType.DMA
    n_sx, n_sy, n_sample = sizes
    sums = (PARTS + 1, PIECE, 128)
    scratch = [
        vm(tile, BF16), vm(tile, BF16), vm(tile, BF16), vm(sums, F32),
        vm((27, CH), F32), vm((1, CH), F32), vm((CH, CH), BF16), vm((CH, CH), BF16),
        vm(field, BF16), vm(field, BF16),
        vm(field, F32), vm(field, F32), vm(field, F32),
        vm(field, F32), vm(field, F32), vm(field, F32),
        vm(pairs, BF16), vm(pairs, F32), vm(pairs, F32),
        vm((28, CH, 128), F32), vm((28, CH, 128), F32),
        vm((CH, CH), BF16), vm((CH, CH), BF16), vm((NC, 2 * NC), BF16), vm((256, 256), BF16),
        vm((4, 16, CH), BF16), vm((4, 16, CH), BF16), vm((6, 4, 16, CH), BF16), vm((6, 4, 16, CH), BF16),
        vm((NR // 2, 8, CH), F32), vm((CH, 128), BF16),
        vm((CH, CH), F32), vm((CH, CH + 16), F32), vm((CH, 128), BF16), vm((28, 8, CH), F32),
        vm((PARTS, PIECE, 128), BF16), vm((PARTS, PIECE, 128), BF16), vm((16, PIECE, 128), BF16),
        vm((PARTS, PIECE, 128), BF16), vm((PIECE, 128), BF16), vm(pairs, BF16),
        vm((CHUNK, 128), BF16), vm((8, CHUNK, 128), BF16), vm((CHUNK, 128), BF16), vm((16, CHUNK, 128), BF16),
        dma((8,)), dma((4,)), dma((2, 12)), dma((2, 12)),
        dma((8,)), dma((8,)), dma((16,)), dma((16,)), dma((8,)), dma((8,)),
        dma((8,)), dma((8,)), dma((16,)), dma((16,)),
    ]
    there = pl.BlockSpec(memory_space=pl.ANY)
    params = dict(vmem_limit_bytes=60 * 1024 * 1024)
    if n_sx > 1:
        params.update(collective_id=0, has_side_effects=True)
    ig, sums = pl.pallas_call(
        functools.partial(kernel, sizes, factor),
        out_shape=(jax.ShapeDtypeStruct(tile, BF16), jax.ShapeDtypeStruct(sums, F32)),
        in_specs=[there] * 6,
        out_specs=(there, there),
        scratch_shapes=scratch,
        compiler_params=pltpu.CompilerParams(**params),
        name="block",
    )(
        inputs.reshape(tile),
        cotangent.reshape(tile),
        depth_kernel.T,
        mix_bias.reshape(1, CH),
        mix_in,
        mix_out,
    )
    ig, kg, mig, bg, mog = pl.pallas_call(
        deliver,
        out_shape=(
            jax.ShapeDtypeStruct(tile, BF16),
            jax.ShapeDtypeStruct((27, CH), F32),
            jax.ShapeDtypeStruct((CH, CH), F32),
            jax.ShapeDtypeStruct((1, CH), F32),
            jax.ShapeDtypeStruct((CH, CH), F32),
        ),
        in_specs=[there] * 2,
        out_specs=(there,) * 5,
        scratch_shapes=[
            vm(tile, BF16), vm(sums.shape, F32), vm((27, CH), F32), vm((CH, CH), F32), vm((1, CH), F32),
            vm((CH, CH), F32), dma((2, 8)),
        ],
        compiler_params=pltpu.CompilerParams(vmem_limit_bytes=60 * 1024 * 1024),
        name="deliver",
    )(ig, sums)
    return (ig.reshape(inputs.shape), kg.T, mig, bg.reshape(CH), mog)


def solution(mesh):
    sizes = tuple(mesh.shape[a] for a in ("sx", "sy", "sample"))
    cells = sizes[0] * sizes[1] * sizes[2] * 2 * NR * NC
    field = P("sample", None, None, "sx", "sy")
    return jax.shard_map(
        functools.partial(per_device, sizes, 1.0 / math.sqrt(cells)),
        mesh=mesh,
        in_specs=(field, field, P(), P(), P(), P()),
        out_specs=(field, P(), P(), P(), P()),
        check_vma=False,
    )
```

```python
import functools
import math

import jax
import jax.numpy as jnp
from jax import lax
from jax.experimental import pallas as pl
from jax.experimental.pallas import tpu as pltpu
from jax.sharding import PartitionSpec as P

INV_SQRT2 = 0.7071067811865476
INV_SQRT2PI = 0.3989422804014327
MESH = pl.DeviceIdType.MESH
F32 = jnp.float32
BF16 = jnp.bfloat16

CH = 192
NR = 16
NC = 128
RR = NR + 2
BLK = 8
WIDE = 16
CHUNK = 48
PIECE = 80
PARTS = 8


def dot(a, b):
    return jnp.dot(a, b, preferred_element_type=F32)


def dot_nt(a, b):
    return lax.dot_general(a, b, (((1,), (1,)), ((), ())), preferred_element_type=F32)


def iota(shape, dim):
    return lax.broadcasted_iota(jnp.int32, shape, dim)


def one_hot(cond):
    return jnp.where(cond, 1.0, 0.0).astype(BF16)


def block_of(b, size):
    return pl.ds(pl.multiple_of(b * size, size), size)


def rim_place(r, z):
    return 4 * r + 2 * z


def swap_sides(packed):
    even = iota(packed.shape, 1) % 2 == 0
    return jnp.where(even, pltpu.roll(packed, 127, axis=1), pltpu.roll(packed, 1, axis=1))


def pick_matrix():
    u = iota((8, 4 * NC), 0)
    k = iota((8, 4 * NC), 1)
    return one_hot(k == (u // 2) * NC + jnp.where(u % 2 == 0, NC - 1, 0))


def rim_matrix(at):
    lane = iota((128, 2 * NC), 0)
    j = iota((128, 2 * NC), 1)
    return one_hot(((j == 0) & (lane == at)) | ((j == 2 * NC - 1) & (lane == at + 1)))


def shift_matrix():
    k = iota((NC, 2 * NC), 0)
    j = iota((NC, 2 * NC), 1)
    return one_hot(((j < NC) & (k == j - 1)) | ((j >= NC) & (k == j - NC + 1)))


def swap_matrix():
    k = iota((256, 256), 0)
    j = iota((256, 256), 1)
    return one_hot((k // 16 == j % 16) & (k % 16 == j // 16))


def tap_matrix(d):
    row = iota((128, 256), 0)
    k = jnp.where(row < 96, row % 32, -2)
    t = 2 * d + jnp.where(iota((128, 256), 1) < 128, 0, 1)
    plus = jnp.where(t < 9, t + 9, jnp.where(t < 18, t + 9, jnp.where(t < 27, t - 18, 27)))
    minus = jnp.where((t < 9) | (t > 26), -1, jnp.where(t < 18, t, t - 9))
    return (jnp.where(k == plus, 1.0, 0.0) - jnp.where(k == minus, 1.0, 0.0)).astype(BF16)


def stencil_block(a0, am, ap, w, flip, rows, emit, first_row=0, last_row=RR - 1):
    k0 = [w[8 - t if flip else t, rows, :] for t in range(9)]
    kp = [w[18 + 8 - t if flip else 9 + t, rows, :] for t in range(9)]
    km = [w[9 + 8 - t if flip else 18 + t, rows, :] for t in range(9)]
    live = {}
    for r in range(first_row, last_row + 1):
        lower = [ref[r, 0, rows, :] for ref in (am, a0, ap)]
        upper = [ref[r, 1, rows, :] for ref in (am, a0, ap)]
        both = [u + v for u, v in zip(lower, upper)]
        for q in (1, 0, -1):
            i = r - 1 - q
            if not 0 <= i < NR:
                continue
            total = live.get(i, [None, None, None])
            for s in range(3):
                t = 3 * (q + 1) + s
                terms = (k0[t] * both[s], kp[t] * upper[s], km[t] * lower[s])
                total = [b if a is None else a + b for a, b in zip(total, terms)]
            live[i] = total
        for i in sorted(live):
            if i + 2 == r or r == last_row:
                shared, first, second = live.pop(i)
                emit(i, shared + first, shared + second)


def near_lanes(packed):
    return {off: pltpu.roll(packed, (128 - off) % 128, axis=1) if off else packed for off in range(-2, 12, 2)}


def tap_sums_block(g0, a0, am, ap, hx, gp, rows):
    near = near_lanes(hx[rows, :])
    grads = gp[rows, :]
    lane = iota((BLK, NC), 1)
    even = lane % 2 == 0
    lower_grads = jnp.where(lane % 4 < 2, grads, 0.0)
    upper_grads = grads - lower_grads
    sums = [jnp.zeros((BLK, NC), F32)] * 27
    for q in range(3):
        up = lower_grads * near[4 * q + 2]
        down = upper_grads * near[4 * q - 2]
        for kind, value in ((0, grads * near[4 * q] + up + down), (1, up), (2, down)):
            left = jnp.where(even, value, 0.0)
            sums[9 * kind + 3 * q] = left
            sums[9 * kind + 3 * q + 2] = value - left

    def step(r, sums):
        sums = list(sums)
        first = g0[r + 1, 0, rows, :]
        second = g0[r + 1, 1, rows, :]
        shared = first + second
        for q in range(3):
            for s, ref in enumerate((am, a0, ap)):
                lower = ref[r + q, 0, rows, :]
                upper = ref[r + q, 1, rows, :]
                t = 3 * q + s
                sums[t] = sums[t] + shared * (lower + upper)
                sums[9 + t] = sums[9 + t] + first * upper
                sums[18 + t] = sums[18 + t] + second * lower
        return tuple(sums)

    sums = lax.fori_loop(0, NR, step, tuple(sums), unroll=8)
    middle = [sums[t] - sums[9 + t] - sums[18 + t] for t in range(9)]
    return list(sums[18:]) + middle + list(sums[9:18])


def kernel(
    sizes, factor,
    x_hbm, cot_hbm, dk_hbm, bias_hbm, mi_hbm, mo_hbm,
    ig_hbm, sums_hbm,
    xv, cv, ov, sums_ref, dk, bias, mi, mo,
    xb, hb, a0, am, ap, b0, bm, bp, cb, ag, hid, w, acc, mit, mot, turn, swap,
    px, ph, prx, prh, edge, halo, hx, fx, gp, fw, moa, mia, tall, flat, gs, ar, br, fin, bs, pgs, ks, kr, kt, kg,
    load, save, hsend, hrecv, asend, arecv, bsend, brecv, csend, crecv, ksend, krecv, lsend, lrecv,
):
    n_sx, n_sy, n_sample = sizes
    comm = n_sx > 1
    n_group = n_sy * n_sample
    sx, sy, sample = (lax.axis_index(a) for a in ("sx", "sy", "sample"))
    me = sy * n_sample + sample

    def at_group(g):
        return {"sx": sx, "sy": g // n_sample, "sample": g % n_sample}

    def around(dx, dy):
        return {
            "sx": lax.rem(sx + dx + n_sx, n_sx),
            "sy": lax.rem(sy + dy + n_sy, n_sy),
            "sample": sample,
        }

    third = CH // 3
    loads = [pltpu.make_async_copy(x_hbm.at[pl.ds(third * k, third)], xv.at[pl.ds(third * k, third)], load.at[k]) for k in range(3)]
    loads += [
        pltpu.make_async_copy(src, dst, load.at[3 + k])
        for k, (src, dst) in enumerate(((mi_hbm, mi), (mo_hbm, mo), (dk_hbm, dk), (bias_hbm, bias), (cot_hbm, cv)))
    ]
    with jax.named_scope("start"):
        for copy in loads[3:7] + loads[:3]:
            copy.start()
        if comm:
            barrier = pltpu.get_barrier_semaphore()
            for d in range(1, n_group):
                pl.semaphore_signal(barrier, inc=1, device_id=at_group(lax.rem(me + d, n_group)), device_id_type=MESH)
            for d in range(1, n_sx):
                pl.semaphore_signal(barrier, inc=1, device_id=around(d, 0), device_id_type=MESH)
            for dx in (-1, 1):
                for dy in (-1, 1):
                    pl.semaphore_signal(barrier, inc=1, device_id=around(dx, dy), device_id_type=MESH)

    pack_to = ((0, 1, 0), (1, 1, 1), (-1, 1, 2), (0, -1, 3), (1, -1, 4), (-1, -1, 5))

    def pack_copy(which, src, dst, slot):
        dx, dy, at = pack_to[slot]
        if dx:
            src, dst = src.at[3 if dx > 0 else 0], dst.at[at, 0]
        else:
            dst = dst.at[at]
        return pltpu.make_async_remote_copy(
            src_ref=src, dst_ref=dst, send_sem=hsend.at[which, at], recv_sem=hrecv.at[which, at],
            device_id=around(dx, dy), device_id_type=MESH,
        )

    def slab_copy(which, ref, up, k):
        part = pl.ds(third * k, third)
        return pltpu.make_async_remote_copy(
            src_ref=ref.at[NR if up else 1, :, part], dst_ref=ref.at[0 if up else NR + 1, :, part],
            send_sem=hsend.at[which, 6 + 3 * up + k], recv_sem=hrecv.at[which, 6 + 3 * up + k],
            device_id=around(1 if up else -1, 0), device_id_type=MESH,
        )

    def pack_edges(sent):
        for k in range(4):
            sent[k] = jnp.concatenate([edge[2 * k], edge[2 * k + 1]], axis=0).astype(BF16)

    def send_edges(which, sent, recv):
        if comm:
            for slot in range(6):
                pack_copy(which, sent, recv, slot).start()

    def rim(recv):
        def piece(slot, block, dx, dy):
            ok = (sx + dx >= 0) & (sx + dx < n_sx) & (sy + dy >= 0) & (sy + dy < n_sy)
            return jnp.where(ok, recv[slot, block].astype(F32), 0.0)

        left = iota((16, CH), 0) % 2 == 0
        tall = [jnp.where(left, piece(0, k, 0, -1), piece(3, k, 0, 1)) for k in range(4)]
        tall.append(jnp.where(left, piece(2, 0, 1, -1), piece(5, 0, 1, 1)))
        tall.append(jnp.zeros((32, CH), F32))
        tall.append(jnp.where(left, piece(1, 0, -1, -1), piece(4, 0, -1, 1)))
        square = jnp.concatenate(tall, axis=0)
        square = jnp.concatenate([square, jnp.zeros((128, 64), F32)], axis=1)
        return pltpu.roll(square.T[:CH], 4, axis=1)

    def edge_lanes():
        square = jnp.concatenate([edge[...].reshape(64, CH), jnp.zeros((64, CH), F32)], axis=0)
        square = jnp.concatenate([square, jnp.zeros((128, 64), F32)], axis=1)
        return square.T[:CH]

    def real_row(rows_ref, r):
        ok = sx > 0 if r == 0 else sx < n_sx - 1
        return jnp.where(ok, rows_ref[r].astype(F32), 0.0).astype(BF16)

    def spread_plain(value, mid, back, ahead, r):
        mid[r] = value.astype(F32)
        both = dot(value.reshape(2 * CH, NC), turn[...])
        back[r] = both[:, :NC].reshape(2, CH, NC)
        ahead[r] = both[:, NC:].reshape(2, CH, NC)

    def spread(rows_ref, mid, back, ahead, r, z):
        value = real_row(rows_ref, r)[z] if isinstance(r, int) else rows_ref[r, z]
        mid[r, z] = value.astype(F32)
        lhs = jnp.concatenate([value, halo[...]], axis=1)
        rhs = jnp.concatenate([turn[...], rim_matrix(rim_place(r, z))], axis=0)
        both = dot(lhs, rhs)
        back[r, z] = both[:, :NC]
        ahead[r, z] = both[:, NC:]

    def spread_all(which, rows_ref, mid, back, ahead, sent, recv):
        if comm:
            for slot in range(6):
                pack_copy(which, sent, recv, slot).wait_recv()
            halo[...] = rim(recv).astype(BF16)
        else:
            halo[...] = jnp.zeros_like(halo)

        @pl.loop(1, NR + 1, unroll=4)
        def _(r):
            for z in range(2):
                spread(rows_ref, mid, back, ahead, r, z)

        if comm:
            for k in range(3):
                slab_copy(which, rows_ref, 0, k).wait_recv()
                slab_copy(which, rows_ref, 1, k).wait_recv()
        else:
            rows_ref[0] = jnp.zeros_like(rows_ref[0])
            rows_ref[NR + 1] = jnp.zeros_like(rows_ref[0])
        for r in (0, NR + 1):
            for z in range(2):
                spread(rows_ref, mid, back, ahead, r, z)

    with jax.named_scope("constants"):
        for k in range(3, 7):
            loads[k].wait()
        turn[...] = shift_matrix()
        swap[...] = swap_matrix()
        eye = one_hot(iota((CH, CH), 0) == iota((CH, CH), 1))
        mit[...] = dot_nt(eye, mi[...]).astype(BF16)
        mot[...] = dot_nt(eye, mo[...]).astype(BF16)

    with jax.named_scope("weights"):
        value = jnp.concatenate([dk[...], bias[...], jnp.zeros((100, CH), F32)], axis=0)
        value = jnp.concatenate([value, jnp.zeros((128, 64), F32)], axis=1).T[:CH]
        high = value.astype(BF16).astype(F32)
        middle = (value - high).astype(BF16).astype(F32)
        low = value - high - middle
        tall[...] = (high + pltpu.roll(middle, 32, axis=1) + pltpu.roll(low, 64, axis=1)).astype(BF16)

        @pl.loop(0, 14, unroll=7)
        def _(d):
            both = dot(tall[...], tap_matrix(d))
            w[2 * d] = both[:, :128]
            w[2 * d + 1] = both[:, 128:]

        even = iota((CH, 128), 1) % 2 == 0
        below = iota((CH, 128), 1) % 4 < 2
        for q in range(3):
            own, up, down = (jnp.where(even, w[9 * k + 3 * q], w[9 * k + 3 * q + 2]) for k in range(3))
            fw[2 * q] = own
            fw[2 * q + 1] = own + jnp.where(below, up, down)

    with jax.named_scope("rows of x"):
        for k in range(3):
            loads[k].wait()

            @pl.loop(4 * k, 4 * k + 4, unroll=4)
            def _(b):
                part = xv[block_of(b, WIDE)]
                rhs = jnp.concatenate([part[:, z].reshape(WIDE * NR, NC) for z in range(2)], axis=1)
                both = dot(swap[...], rhs).astype(BF16)
                for i in range(NR):
                    for z in range(2):
                        xb[i + 1, z, block_of(b, WIDE), :] = both[WIDE * i : WIDE * (i + 1), NC * z : NC * (z + 1)]

            if comm:
                if k == 0:
                    pl.semaphore_wait(barrier, n_group - 1 + n_sx - 1 + 4)
                slab_copy(0, xb, 0, k).start()
                slab_copy(0, xb, 1, k).start()
        loads[7].start()

    with jax.named_scope("send x"):
        pick = pick_matrix()
        for i in range(NR // 2):
            four = jnp.concatenate([xb[2 * i + 1 + k // 2, k % 2] for k in range(4)], axis=1)
            edge[i] = dot_nt(pick, four)
        pack_edges(px)
        send_edges(0, px, prx)

    with jax.named_scope("spread x"):
        @pl.loop(1, NR + 1, unroll=8)
        def _(r):
            spread_plain(xb[r], a0, am, ap, r)

    loads[7].wait()
    with jax.named_scope("cotangent"):
        @pl.loop(0, CH // WIDE, unroll=12)
        def _(b):
            part = cv[block_of(b, WIDE)]
            rhs = jnp.concatenate([part[:, z].reshape(WIDE * NR, NC) for z in range(2)], axis=1)
            both = dot(swap[...], rhs).astype(BF16)
            for i in range(NR):
                cb[i // 2, block_of(b, WIDE), 256 * (i % 2) : 256 * (i % 2) + 256] = both[WIDE * i : WIDE * (i + 1)]

    with jax.named_scope("hidden"):
        @pl.loop(0, CH // BLK)
        def _(b):
            rows = block_of(b, BLK)

            def emit(i, first, second):
                at = 256 * (i % 2)
                hid[i // 2, rows, at : at + 128] = first
                hid[i // 2, rows, at + 128 : at + 256] = second

            stencil_block(a0, am, ap, w, False, rows, emit, 1, NR)

    with jax.named_scope("halo x"):
        if comm:
            for slot in range(6):
                pack_copy(0, px, prx, slot).wait_recv()
            hx[...] = rim(prx)
            for k in range(3):
                slab_copy(0, xb, 0, k).wait_recv()
                slab_copy(0, xb, 1, k).wait_recv()
        else:
            hx[...] = jnp.zeros_like(hx)
            xb[0] = jnp.zeros_like(xb[0])
            xb[NR + 1] = jnp.zeros_like(xb[0])
        for r in (0, NR + 1):
            spread_plain(real_row(xb, r), a0, am, ap, r)

        @pl.loop(0, CH // BLK, unroll=4)
        def _(b):
            rows = block_of(b, BLK)
            for r, i, t0 in ((0, 0, 0), (NR + 1, NR - 1, 6)):
                shared, first, second = 0.0, 0.0, 0.0
                for s, ref in enumerate((am, a0, ap)):
                    lower = ref[r, 0, rows, :]
                    upper = ref[r, 1, rows, :]
                    shared = shared + w[t0 + s, rows, :] * (lower + upper)
                    first = first + w[9 + t0 + s, rows, :] * upper
                    second = second + w[18 + t0 + s, rows, :] * lower
                at = 256 * (i % 2)
                hid[i // 2, rows, at : at + 128] += shared + first
                hid[i // 2, rows, at + 128 : at + 256] += shared + second

            below = iota((BLK, 128), 1) % 4 < 2
            near = near_lanes(hx[rows, :])
            total = 0.0
            for q in range(3):
                total = total + fw[2 * q, rows, :] * near[4 * q]
                total = total + fw[2 * q + 1, rows, :] * jnp.where(below, near[4 * q + 2], near[4 * q - 2])
            fx[rows, :] = swap_sides(total)

    with jax.named_scope("chain"):
        moa[...] = jnp.zeros_like(moa)
        mia[...] = jnp.zeros_like(mia)

        @pl.loop(0, NR // 2, unroll=8)
        def _(i):
            column = iota((CH, NC), 1)
            outer = (column == 0) | (column == NC - 1)
            hidden = []
            for k in range(4):
                add = jnp.where(outer, pltpu.roll(fx[...], NC - 1 - 8 * i - 2 * k, axis=1), 0.0)
                hidden.append((hid[i, :, NC * k : NC * (k + 1)] + add).astype(BF16))
            hidden = jnp.concatenate(hidden, axis=1)
            shift = w[27]
            pre = dot(mi[...], hidden) + jnp.concatenate([shift] * 4, axis=1)
            cdf = 0.5 * (1.0 + lax.erf(pre * INV_SQRT2))
            dens = jnp.exp(-0.5 * pre * pre) * INV_SQRT2PI
            act = (pre * cdf).astype(BF16)
            pg = (dot(mot[...], cb[i]) * (cdf + pre * dens)).astype(BF16)
            moa[...] += dot_nt(cb[i], act)
            mia[...] += dot_nt(pg, jnp.concatenate([hidden, jnp.ones((16, 4 * NC), BF16)], axis=0))
            pgs[i] = pg

    def over_sx(src, dst, sends, recvs, d):
        return pltpu.make_async_remote_copy(
            src_ref=src, dst_ref=dst.at[sx], send_sem=sends.at[d], recv_sem=recvs.at[sx],
            device_id=around(d, 0), device_id_type=MESH,
        )

    def over_group(src, dst, sends, recvs, d):
        return pltpu.make_async_remote_copy(
            src_ref=src, dst_ref=dst.at[me], send_sem=sends.at[d], recv_sem=recvs.at[me],
            device_id=at_group(lax.rem(me + d, n_group)), device_id_type=MESH,
        )

    def scatter(d):
        return over_sx(gs.at[lax.rem(sx + d, n_sx)], ar, asend, arecv, d)

    def publish(d):
        return over_sx(fin.at[sx], fin, csend, crecv, d)

    def arrived(ref, sem, slot):
        pltpu.make_async_remote_copy(
            src_ref=ref.at[slot], dst_ref=ref.at[slot], send_sem=asend.at[0], recv_sem=sem.at[slot],
            device_id=around(1, 0), device_id_type=MESH,
        ).wait_recv()

    def arrived_sx(ref, sem):
        for d in range(1, n_sx):
            arrived(ref, sem, lax.rem(sx + d, n_sx))

    def arrived_group(ref, sem):
        for d in range(1, n_group):
            arrived(ref, sem, lax.rem(me + d, n_group))

    def added(ref, count):
        total = ref[0].astype(F32)
        for k in range(1, count):
            total = total + ref[k].astype(F32)
        return total

    def sum_sx():
        if comm:
            arrived_sx(ar, arecv)
            ar[sx] = gs[sx]
            bs[...] = added(ar, n_sx).astype(BF16)
            for d in range(1, n_group):
                over_group(bs, br, bsend, brecv, d).start()
            br[me] = bs[...]

    def sum_group():
        if comm:
            arrived_group(br, brecv)
            fin[sx] = added(br, n_group).astype(BF16)
            for d in range(1, n_sx):
                publish(d).start()

    def sum_taps():
        if comm:
            arrived_sx(kr, krecv)
            kr[sx] = ks[...]
            kt[...] = added(kr, n_sx).astype(BF16)
            for d in range(1, n_group):
                over_group(kt, kg, lsend, lrecv, d).start()
            kg[me] = kt[...]

    with jax.named_scope("scatter mixes"):
        for k in range(PARTS):
            at = pl.ds(24 * k, 24)
            mid = jnp.concatenate([moa[at, 128:192], mia[at, 0:64]], axis=1)
            value = jnp.concatenate([moa[at, 0:128], mid, mia[at, 64:192], jnp.zeros((8, 128), F32)], axis=0)
            gs[k] = value.astype(BF16)
        if comm:
            for d in range(1, n_sx):
                scatter(d).start()

    with jax.named_scope("hidden grad"):
        @pl.loop(0, NR // 2, unroll=8)
        def _(i):
            hg = dot(mit[...], pgs[i]).astype(BF16)
            for k in range(4):
                piece = hg[:, NC * k : NC * (k + 1)]
                hb[2 * i + 1 + k // 2, k % 2] = piece
                b0[2 * i + 1 + k // 2, k % 2] = piece.astype(F32)
            edge[i] = dot_nt(pick_matrix(), hg)

    with jax.named_scope("send grad"):
        if comm:
            for k in range(3):
                slab_copy(1, hb, 0, k).start()
                slab_copy(1, hb, 1, k).start()
        pack_edges(ph)
        send_edges(1, ph, prh)

    def tap_sums(start, stop):
        @pl.loop(start, stop)
        def _(b):
            rows = block_of(b, BLK)
            for k, value in enumerate(tap_sums_block(b0, a0, am, ap, hx, gp, rows)):
                acc[k, rows, :] = value

    with jax.named_scope("tap sums"):
        gp[...] = swap_sides(edge_lanes())
        tap_sums(0, 20)
    with jax.named_scope("sum sx"):
        sum_sx()
    with jax.named_scope("tap sums 2"):
        tap_sums(20, 24)
        acc[27] = jnp.where(iota((CH, NC), 1) == 0, mia[:, 192:193], 0.0)

        for k in range(28):
            value = acc[k]
            high = value.astype(BF16)
            low = (value - high.astype(F32)).astype(BF16)
            flat[k] = dot_nt(jnp.ones((8, 2 * NC), BF16), jnp.concatenate([high, low], axis=1))

    with jax.named_scope("scatter taps"):
        value = jnp.concatenate([flat[k, 0:1] for k in range(28)] + [jnp.zeros((4, CH), F32)], axis=0)
        ks[0:32] = value[:, 0:128].astype(BF16)
        ks[32:48] = jnp.concatenate([value[0:16, 128:192], value[16:32, 128:192]], axis=1).astype(BF16)
        if comm:
            for d in range(1, n_sx):
                over_sx(ks, kr, ksend, krecv, d).start()

    with jax.named_scope("spread grad"):
        spread_all(1, hb, b0, bm, bp, ph, prh)

    def input_grad(start, stop):
        @pl.loop(2 * start, 2 * stop)
        def _(b):
            rows = block_of(b, BLK)

            def emit(i, first, second):
                at = 256 * (i % 2)
                ag[i // 2, rows, at : at + 128] = first
                ag[i // 2, rows, at + 128 : at + 256] = second

            stencil_block(b0, bm, bp, w, True, rows, emit)

        @pl.loop(start, stop, unroll=stop - start)
        def _(b):
            rows = block_of(b, WIDE)
            rhs = [ag[i // 2, rows, 256 * (i % 2) : 256 * (i % 2) + 256].astype(BF16) for i in range(NR)]
            both = dot(swap[...], jnp.concatenate(rhs, axis=0))
            for z in range(2):
                value = both[:, NC * z : NC * (z + 1)].reshape(WIDE, NR, NC)
                ov[rows, z] = (cv[rows, z].astype(F32) + value).astype(BF16)

    def save_part(part):
        at = pl.ds(third * part, third)
        return pltpu.make_async_copy(ov.at[at], ig_hbm.at[at], save.at[part])

    with jax.named_scope("grad 1"):
        input_grad(0, 3)
    with jax.named_scope("sum rest"):
        sum_taps()
    with jax.named_scope("grad 2"):
        input_grad(3, 5)
    with jax.named_scope("sum rest 2"):
        sum_group()
    with jax.named_scope("grad 3"):
        input_grad(5, 8)
    save_part(0).start()
    save_part(1).start()
    with jax.named_scope("grad 4"):
        input_grad(8, 12)
    save_part(2).start()

    with jax.named_scope("finish"):
        if comm:
            for which, rows_ref, sent, recv in ((0, xb, px, prx), (1, hb, ph, prh)):
                for slot in range(6):
                    pack_copy(which, sent, recv, slot).wait_send()
                for k in range(3):
                    slab_copy(which, rows_ref, 0, k).wait_send()
                    slab_copy(which, rows_ref, 1, k).wait_send()
            for d in range(1, n_sx):
                scatter(d).wait_send()
                over_sx(ks, kr, ksend, krecv, d).wait_send()
                publish(d).wait_send()
            for d in range(1, n_group):
                over_group(bs, br, bsend, brecv, d).wait_send()
                over_group(kt, kg, lsend, lrecv, d).wait_send()
            arrived_sx(fin, crecv)
            arrived_group(kg, lrecv)
            sums_ref[PARTS, 0:CHUNK] = added(kg, n_group) * factor
        else:
            fin[...] = gs[...]
            sums_ref[PARTS, 0:CHUNK] = ks[...].astype(F32) * factor
        sums_ref[PARTS, CHUNK:PIECE] = jnp.zeros((PIECE - CHUNK, 128), F32)
        sums_ref[0:PARTS] = fin[...].astype(F32) * factor
        last = pltpu.make_async_copy(sums_ref, sums_hbm, save.at[3])
        last.start()
        for part in range(3):
            save_part(part).wait()
        last.wait()


def deliver(ig_in, sums_in, ig_out, kg_out, mig_out, bg_out, mog_out, held, sums, kg, mig, bg, mog, sems):
    parts = CH // 4
    at = [pl.ds(parts * k, parts) for k in range(4)]
    inward = [pltpu.make_async_copy(ig_in.at[at[k]], held.at[at[k]], sems.at[0, k]) for k in range(4)]
    outward = [pltpu.make_async_copy(held.at[at[k]], ig_out.at[at[k]], sems.at[1, k]) for k in range(4)]
    first = pltpu.make_async_copy(sums_in, sums, sems.at[0, 4])
    first.start()
    for copy in inward:
        copy.start()
    first.wait()
    for k in range(PARTS):
        rows = pl.ds(24 * k, 24)
        mog[rows, 0:128] = sums[k, 0:24]
        mog[rows, 128:192] = sums[k, 24:48, 0:64]
        mig[rows, 0:64] = sums[k, 24:48, 64:128]
        mig[rows, 64:192] = sums[k, 48:72]
    kg[:, 0:128] = sums[PARTS, 0:27]
    kg[0:16, 128:192] = sums[PARTS, 32:48, 0:64]
    kg[16:27, 128:192] = sums[PARTS, 32:43, 64:128]
    bg[:, 0:128] = sums[PARTS, 27:28]
    bg[:, 128:192] = sums[PARTS, 43:44, 64:128]
    pairs = ((kg, kg_out), (mig, mig_out), (bg, bg_out), (mog, mog_out))
    small = [pltpu.make_async_copy(src, dst, sems.at[1, 4 + k]) for k, (src, dst) in enumerate(pairs)]
    for copy in small:
        copy.start()
    for k in range(4):
        inward[k].wait()
        outward[k].start()
    for copy in outward + small:
        copy.wait()


def per_device(sizes, factor, inputs, cotangent, depth_kernel, mix_in, mix_bias, mix_out):
    tile = (CH, 2, NR, NC)
    vm = pltpu.VMEM
    field = (RR, 2, CH, NC)
    pairs = (NR // 2, CH, 4 * NC)
    dma = pltpu.SemaphoreType.DMA
    n_sx, n_sy, n_sample = sizes
    sums = (PARTS + 1, PIECE, 128)
    scratch = [
        vm(tile, BF16), vm(tile, BF16), vm(tile, BF16), vm(sums, F32),
        vm((27, CH), F32), vm((1, CH), F32), vm((CH, CH), BF16), vm((CH, CH), BF16),
        vm(field, BF16), vm(field, BF16),
        vm(field, F32), vm(field, F32), vm(field, F32),
        vm(field, F32), vm(field, F32), vm(field, F32),
        vm(pairs, BF16), vm(pairs, F32), vm(pairs, F32),
        vm((28, CH, 128), F32), vm((28, CH, 128), F32),
        vm((CH, CH), BF16), vm((CH, CH), BF16), vm((NC, 2 * NC), BF16), vm((256, 256), BF16),
        vm((4, 16, CH), BF16), vm((4, 16, CH), BF16), vm((6, 4, 16, CH), BF16), vm((6, 4, 16, CH), BF16),
        vm((NR // 2, 8, CH), F32), vm((CH, 128), BF16),
        vm((CH, 128), F32), vm((CH, 128), F32), vm((CH, 128), F32), vm((6, CH, 128), F32),
        vm((CH, CH), F32), vm((CH, CH + 16), F32), vm((CH, 128), BF16), vm((28, 8, CH), F32),
        vm((PARTS, PIECE, 128), BF16), vm((PARTS, PIECE, 128), BF16), vm((16, PIECE, 128), BF16),
        vm((PARTS, PIECE, 128), BF16), vm((PIECE, 128), BF16), vm(pairs, BF16),
        vm((CHUNK, 128), BF16), vm((8, CHUNK, 128), BF16), vm((CHUNK, 128), BF16), vm((16, CHUNK, 128), BF16),
        dma((8,)), dma((4,)), dma((2, 12)), dma((2, 12)),
        dma((8,)), dma((8,)), dma((16,)), dma((16,)), dma((8,)), dma((8,)),
        dma((8,)), dma((8,)), dma((16,)), dma((16,)),
    ]
    there = pl.BlockSpec(memory_space=pl.ANY)
    params = dict(vmem_limit_bytes=60 * 1024 * 1024)
    if n_sx > 1:
        params.update(collective_id=0, has_side_effects=True)
    ig, sums = pl.pallas_call(
        functools.partial(kernel, sizes, factor),
        out_shape=(jax.ShapeDtypeStruct(tile, BF16), jax.ShapeDtypeStruct(sums, F32)),
        in_specs=[there] * 6,
        out_specs=(there, there),
        scratch_shapes=scratch,
        compiler_params=pltpu.CompilerParams(**params),
        name="block",
    )(
        inputs.reshape(tile),
        cotangent.reshape(tile),
        depth_kernel.T,
        mix_bias.reshape(1, CH),
        mix_in,
        mix_out,
    )
    ig, kg, mig, bg, mog = pl.pallas_call(
        deliver,
        out_shape=(
            jax.ShapeDtypeStruct(tile, BF16),
            jax.ShapeDtypeStruct((27, CH), F32),
            jax.ShapeDtypeStruct((CH, CH), F32),
            jax.ShapeDtypeStruct((1, CH), F32),
            jax.ShapeDtypeStruct((CH, CH), F32),
        ),
        in_specs=[there] * 2,
        out_specs=(there,) * 5,
        scratch_shapes=[
            vm(tile, BF16), vm(sums.shape, F32), vm((27, CH), F32), vm((CH, CH), F32), vm((1, CH), F32),
            vm((CH, CH), F32), dma((2, 8)),
        ],
        compiler_params=pltpu.CompilerParams(vmem_limit_bytes=60 * 1024 * 1024),
        name="deliver",
    )(ig, sums)
    return (ig.reshape(inputs.shape), kg.T, mig, bg.reshape(CH), mog)


def solution(mesh):
    sizes = tuple(mesh.shape[a] for a in ("sx", "sy", "sample"))
    cells = sizes[0] * sizes[1] * sizes[2] * 2 * NR * NC
    field = P("sample", None, None, "sx", "sy")
    return jax.shard_map(
        functools.partial(per_device, sizes, 1.0 / math.sqrt(cells)),
        mesh=mesh,
        in_specs=(field, field, P(), P(), P(), P()),
        out_specs=(field, P(), P(), P(), P()),
        check_vma=False,
    )
```

```python
import functools
import math

import jax
import jax.numpy as jnp
from jax import lax
from jax.experimental import pallas as pl
from jax.experimental.pallas import tpu as pltpu
from jax.sharding import PartitionSpec as P

INV_SQRT2 = 0.7071067811865476
INV_SQRT2PI = 0.3989422804014327
MESH = pl.DeviceIdType.MESH
F32 = jnp.float32
BF16 = jnp.bfloat16

CH = 192
NR = 16
NC = 128
RR = NR + 2
BLK = 8
WIDE = 16
CHUNK = 48
PIECE = 80
PARTS = 8


def dot(a, b):
    return jnp.dot(a, b, preferred_element_type=F32)


def dot_nt(a, b):
    return lax.dot_general(a, b, (((1,), (1,)), ((), ())), preferred_element_type=F32)


def iota(shape, dim):
    return lax.broadcasted_iota(jnp.int32, shape, dim)


def one_hot(cond):
    return jnp.where(cond, 1.0, 0.0).astype(BF16)


def block_of(b, size):
    return pl.ds(pl.multiple_of(b * size, size), size)


def rim_place(r, z):
    return 4 * r + 2 * z


def swap_sides(packed):
    even = iota(packed.shape, 1) % 2 == 0
    return jnp.where(even, pltpu.roll(packed, 127, axis=1), pltpu.roll(packed, 1, axis=1))


def pick_matrix():
    u = iota((8, 4 * NC), 0)
    k = iota((8, 4 * NC), 1)
    return one_hot(k == (u // 2) * NC + jnp.where(u % 2 == 0, NC - 1, 0))


def rim_matrix(at):
    lane = iota((128, 2 * NC), 0)
    j = iota((128, 2 * NC), 1)
    return one_hot(((j == 0) & (lane == at)) | ((j == 2 * NC - 1) & (lane == at + 1)))


def shift_matrix():
    k = iota((NC, 2 * NC), 0)
    j = iota((NC, 2 * NC), 1)
    return one_hot(((j < NC) & (k == j - 1)) | ((j >= NC) & (k == j - NC + 1)))


def swap_matrix():
    k = iota((256, 256), 0)
    j = iota((256, 256), 1)
    return one_hot((k // 16 == j % 16) & (k % 16 == j // 16))


def tap_matrix(d):
    row = iota((128, 256), 0)
    k = jnp.where(row < 96, row % 32, -2)
    t = 2 * d + jnp.where(iota((128, 256), 1) < 128, 0, 1)
    plus = jnp.where(t < 9, t + 9, jnp.where(t < 18, t + 9, jnp.where(t < 27, t - 18, 27)))
    minus = jnp.where((t < 9) | (t > 26), -1, jnp.where(t < 18, t, t - 9))
    return (jnp.where(k == plus, 1.0, 0.0) - jnp.where(k == minus, 1.0, 0.0)).astype(BF16)


def stencil_block(a0, am, ap, w, flip, rows, emit, first_row=0, last_row=RR - 1):
    k0 = [w[8 - t if flip else t, rows, :] for t in range(9)]
    kp = [w[18 + 8 - t if flip else 9 + t, rows, :] for t in range(9)]
    km = [w[9 + 8 - t if flip else 18 + t, rows, :] for t in range(9)]
    live = {}
    for r in range(first_row, last_row + 1):
        lower = [ref[r, 0, rows, :] for ref in (am, a0, ap)]
        upper = [ref[r, 1, rows, :] for ref in (am, a0, ap)]
        both = [u + v for u, v in zip(lower, upper)]
        for q in (1, 0, -1):
            i = r - 1 - q
            if not 0 <= i < NR:
                continue
            total = live.get(i, [None, None, None])
            for s in range(3):
                t = 3 * (q + 1) + s
                terms = (k0[t] * both[s], kp[t] * upper[s], km[t] * lower[s])
                total = [b if a is None else a + b for a, b in zip(total, terms)]
            live[i] = total
        for i in sorted(live):
            if i + 2 == r or r == last_row:
                shared, first, second = live.pop(i)
                emit(i, shared + first, shared + second)


def near_lanes(packed):
    return {off: pltpu.roll(packed, (128 - off) % 128, axis=1) if off else packed for off in range(-2, 12, 2)}


def tap_sums_block(g0, a0, am, ap, hx, gp, rows):
    near = near_lanes(hx[rows, :])
    grads = gp[rows, :]
    lane = iota((BLK, NC), 1)
    even = lane % 2 == 0
    lower_grads = jnp.where(lane % 4 < 2, grads, 0.0)
    upper_grads = grads - lower_grads
    sums = [jnp.zeros((BLK, NC), F32)] * 27
    for q in range(3):
        up = lower_grads * near[4 * q + 2]
        down = upper_grads * near[4 * q - 2]
        for kind, value in ((0, grads * near[4 * q] + up + down), (1, up), (2, down)):
            left = jnp.where(even, value, 0.0)
            sums[9 * kind + 3 * q] = left
            sums[9 * kind + 3 * q + 2] = value - left

    def step(r, sums):
        sums = list(sums)
        first = g0[r + 1, 0, rows, :]
        second = g0[r + 1, 1, rows, :]
        shared = first + second
        for q in range(3):
            for s, ref in enumerate((am, a0, ap)):
                lower = ref[r + q, 0, rows, :]
                upper = ref[r + q, 1, rows, :]
                t = 3 * q + s
                sums[t] = sums[t] + shared * (lower + upper)
                sums[9 + t] = sums[9 + t] + first * upper
                sums[18 + t] = sums[18 + t] + second * lower
        return tuple(sums)

    sums = lax.fori_loop(0, NR, step, tuple(sums), unroll=8)
    middle = [sums[t] - sums[9 + t] - sums[18 + t] for t in range(9)]
    return list(sums[18:]) + middle + list(sums[9:18])


def kernel(
    sizes,
    x_hbm, cot_hbm, dk_hbm, bias_hbm, mi_hbm, mo_hbm,
    ig_hbm, fin, kg,
    xv, cv, ov, dk, bias, mi, mo,
    xb, hb, a0, am, ap, b0, bm, bp, cb, ag, hid, w, acc, mit, mot, turn, swap,
    px, ph, prx, prh, edge, halo, hx, fx, gp, fw, moa, mia, tall, flat, gs, ar, br, fo, bs, pgs, ks, kr, kt,
    load, save, hsend, hrecv, asend, arecv, bsend, brecv, csend, crecv, ksend, krecv, lsend, lrecv,
):
    n_sx, n_sy, n_sample = sizes
    comm = n_sx > 1
    n_group = n_sy * n_sample
    sx, sy, sample = (lax.axis_index(a) for a in ("sx", "sy", "sample"))
    me = sy * n_sample + sample

    def at_group(g):
        return {"sx": sx, "sy": g // n_sample, "sample": g % n_sample}

    def around(dx, dy):
        return {
            "sx": lax.rem(sx + dx + n_sx, n_sx),
            "sy": lax.rem(sy + dy + n_sy, n_sy),
            "sample": sample,
        }

    third = CH // 3
    loads = [pltpu.make_async_copy(x_hbm.at[pl.ds(third * k, third)], xv.at[pl.ds(third * k, third)], load.at[k]) for k in range(3)]
    loads += [
        pltpu.make_async_copy(src, dst, load.at[3 + k])
        for k, (src, dst) in enumerate(((mi_hbm, mi), (mo_hbm, mo), (dk_hbm, dk), (bias_hbm, bias), (cot_hbm, cv)))
    ]
    with jax.named_scope("start"):
        for copy in loads[3:7] + loads[:3]:
            copy.start()
        if comm:
            barrier = pltpu.get_barrier_semaphore()
            for d in range(1, n_group):
                pl.semaphore_signal(barrier, inc=1, device_id=at_group(lax.rem(me + d, n_group)), device_id_type=MESH)
            for d in range(1, n_sx):
                pl.semaphore_signal(barrier, inc=1, device_id=around(d, 0), device_id_type=MESH)
            for dx in (-1, 1):
                for dy in (-1, 1):
                    pl.semaphore_signal(barrier, inc=1, device_id=around(dx, dy), device_id_type=MESH)

    pack_to = ((0, 1, 0), (1, 1, 1), (-1, 1, 2), (0, -1, 3), (1, -1, 4), (-1, -1, 5))

    def pack_copy(which, src, dst, slot):
        dx, dy, at = pack_to[slot]
        if dx:
            src, dst = src.at[3 if dx > 0 else 0], dst.at[at, 0]
        else:
            dst = dst.at[at]
        return pltpu.make_async_remote_copy(
            src_ref=src, dst_ref=dst, send_sem=hsend.at[which, at], recv_sem=hrecv.at[which, at],
            device_id=around(dx, dy), device_id_type=MESH,
        )

    def slab_copy(which, ref, up, k):
        part = pl.ds(third * k, third)
        return pltpu.make_async_remote_copy(
            src_ref=ref.at[NR if up else 1, :, part], dst_ref=ref.at[0 if up else NR + 1, :, part],
            send_sem=hsend.at[which, 6 + 3 * up + k], recv_sem=hrecv.at[which, 6 + 3 * up + k],
            device_id=around(1 if up else -1, 0), device_id_type=MESH,
        )

    def pack_edges(sent):
        for k in range(4):
            sent[k] = jnp.concatenate([edge[2 * k], edge[2 * k + 1]], axis=0).astype(BF16)

    def send_edges(which, sent, recv):
        if comm:
            for slot in range(6):
                pack_copy(which, sent, recv, slot).start()

    def rim(recv):
        def piece(slot, block, dx, dy):
            ok = (sx + dx >= 0) & (sx + dx < n_sx) & (sy + dy >= 0) & (sy + dy < n_sy)
            return jnp.where(ok, recv[slot, block].astype(F32), 0.0)

        left = iota((16, CH), 0) % 2 == 0
        tall = [jnp.where(left, piece(0, k, 0, -1), piece(3, k, 0, 1)) for k in range(4)]
        tall.append(jnp.where(left, piece(2, 0, 1, -1), piece(5, 0, 1, 1)))
        tall.append(jnp.zeros((32, CH), F32))
        tall.append(jnp.where(left, piece(1, 0, -1, -1), piece(4, 0, -1, 1)))
        square = jnp.concatenate(tall, axis=0)
        square = jnp.concatenate([square, jnp.zeros((128, 64), F32)], axis=1)
        return pltpu.roll(square.T[:CH], 4, axis=1)

    def edge_lanes():
        square = jnp.concatenate([edge[...].reshape(64, CH), jnp.zeros((64, CH), F32)], axis=0)
        square = jnp.concatenate([square, jnp.zeros((128, 64), F32)], axis=1)
        return square.T[:CH]

    def real_row(rows_ref, r):
        ok = sx > 0 if r == 0 else sx < n_sx - 1
        return jnp.where(ok, rows_ref[r].astype(F32), 0.0).astype(BF16)

    def spread_plain(value, mid, back, ahead, r):
        mid[r] = value.astype(F32)
        both = dot(value.reshape(2 * CH, NC), turn[...])
        back[r] = both[:, :NC].reshape(2, CH, NC)
        ahead[r] = both[:, NC:].reshape(2, CH, NC)

    def spread(rows_ref, mid, back, ahead, r, z):
        value = real_row(rows_ref, r)[z] if isinstance(r, int) else rows_ref[r, z]
        mid[r, z] = value.astype(F32)
        lhs = jnp.concatenate([value, halo[...]], axis=1)
        rhs = jnp.concatenate([turn[...], rim_matrix(rim_place(r, z))], axis=0)
        both = dot(lhs, rhs)
        back[r, z] = both[:, :NC]
        ahead[r, z] = both[:, NC:]

    def spread_all(which, rows_ref, mid, back, ahead, sent, recv):
        if comm:
            for slot in range(6):
                pack_copy(which, sent, recv, slot).wait_recv()
            halo[...] = rim(recv).astype(BF16)
        else:
            halo[...] = jnp.zeros_like(halo)

        @pl.loop(1, NR + 1, unroll=4)
        def _(r):
            for z in range(2):
                spread(rows_ref, mid, back, ahead, r, z)

        if comm:
            for k in range(3):
                slab_copy(which, rows_ref, 0, k).wait_recv()
                slab_copy(which, rows_ref, 1, k).wait_recv()
        else:
            rows_ref[0] = jnp.zeros_like(rows_ref[0])
            rows_ref[NR + 1] = jnp.zeros_like(rows_ref[0])
        for r in (0, NR + 1):
            for z in range(2):
                spread(rows_ref, mid, back, ahead, r, z)

    with jax.named_scope("constants"):
        for k in range(3, 7):
            loads[k].wait()
        turn[...] = shift_matrix()
        swap[...] = swap_matrix()
        eye = one_hot(iota((CH, CH), 0) == iota((CH, CH), 1))
        mit[...] = dot_nt(eye, mi[...]).astype(BF16)
        mot[...] = dot_nt(eye, mo[...]).astype(BF16)

    with jax.named_scope("weights"):
        value = jnp.concatenate([dk[...], bias[...], jnp.zeros((100, CH), F32)], axis=0)
        value = jnp.concatenate([value, jnp.zeros((128, 64), F32)], axis=1).T[:CH]
        high = value.astype(BF16).astype(F32)
        middle = (value - high).astype(BF16).astype(F32)
        low = value - high - middle
        tall[...] = (high + pltpu.roll(middle, 32, axis=1) + pltpu.roll(low, 64, axis=1)).astype(BF16)

        @pl.loop(0, 14, unroll=7)
        def _(d):
            both = dot(tall[...], tap_matrix(d))
            w[2 * d] = both[:, :128]
            w[2 * d + 1] = both[:, 128:]

        even = iota((CH, 128), 1) % 2 == 0
        below = iota((CH, 128), 1) % 4 < 2
        for q in range(3):
            own, up, down = (jnp.where(even, w[9 * k + 3 * q], w[9 * k + 3 * q + 2]) for k in range(3))
            fw[2 * q] = own
            fw[2 * q + 1] = own + jnp.where(below, up, down)

    with jax.named_scope("rows of x"):
        for k in range(3):
            loads[k].wait()

            @pl.loop(4 * k, 4 * k + 4, unroll=4)
            def _(b):
                part = xv[block_of(b, WIDE)]
                rhs = jnp.concatenate([part[:, z].reshape(WIDE * NR, NC) for z in range(2)], axis=1)
                both = dot(swap[...], rhs).astype(BF16)
                for i in range(NR):
                    for z in range(2):
                        xb[i + 1, z, block_of(b, WIDE), :] = both[WIDE * i : WIDE * (i + 1), NC * z : NC * (z + 1)]

            if comm:
                if k == 0:
                    pl.semaphore_wait(barrier, n_group - 1 + n_sx - 1 + 4)
                slab_copy(0, xb, 0, k).start()
                slab_copy(0, xb, 1, k).start()
        loads[7].start()

    with jax.named_scope("send x"):
        pick = pick_matrix()
        for i in range(NR // 2):
            four = jnp.concatenate([xb[2 * i + 1 + k // 2, k % 2] for k in range(4)], axis=1)
            edge[i] = dot_nt(pick, four)
        pack_edges(px)
        send_edges(0, px, prx)

    with jax.named_scope("spread x"):
        @pl.loop(1, NR + 1, unroll=8)
        def _(r):
            spread_plain(xb[r], a0, am, ap, r)

    loads[7].wait()
    with jax.named_scope("cotangent"):
        @pl.loop(0, CH // WIDE, unroll=12)
        def _(b):
            part = cv[block_of(b, WIDE)]
            rhs = jnp.concatenate([part[:, z].reshape(WIDE * NR, NC) for z in range(2)], axis=1)
            both = dot(swap[...], rhs).astype(BF16)
            for i in range(NR):
                cb[i // 2, block_of(b, WIDE), 256 * (i % 2) : 256 * (i % 2) + 256] = both[WIDE * i : WIDE * (i + 1)]

    with jax.named_scope("hidden"):
        @pl.loop(0, CH // BLK)
        def _(b):
            rows = block_of(b, BLK)

            def emit(i, first, second):
                at = 256 * (i % 2)
                hid[i // 2, rows, at : at + 128] = first
                hid[i // 2, rows, at + 128 : at + 256] = second

            stencil_block(a0, am, ap, w, False, rows, emit, 1, NR)

    with jax.named_scope("halo x"):
        if comm:
            for slot in range(6):
                pack_copy(0, px, prx, slot).wait_recv()
            hx[...] = rim(prx)
            for k in range(3):
                slab_copy(0, xb, 0, k).wait_recv()
                slab_copy(0, xb, 1, k).wait_recv()
        else:
            hx[...] = jnp.zeros_like(hx)
            xb[0] = jnp.zeros_like(xb[0])
            xb[NR + 1] = jnp.zeros_like(xb[0])
        for r in (0, NR + 1):
            spread_plain(real_row(xb, r), a0, am, ap, r)

        @pl.loop(0, CH // BLK, unroll=8)
        def _(b):
            rows = block_of(b, BLK)
            for r, i, t0 in ((0, 0, 0), (NR + 1, NR - 1, 6)):
                shared, first, second = 0.0, 0.0, 0.0
                for s, ref in enumerate((am, a0, ap)):
                    lower = ref[r, 0, rows, :]
                    upper = ref[r, 1, rows, :]
                    shared = shared + w[t0 + s, rows, :] * (lower + upper)
                    first = first + w[9 + t0 + s, rows, :] * upper
                    second = second + w[18 + t0 + s, rows, :] * lower
                at = 256 * (i % 2)
                hid[i // 2, rows, at : at + 128] += shared + first
                hid[i // 2, rows, at + 128 : at + 256] += shared + second

            below = iota((BLK, 128), 1) % 4 < 2
            near = near_lanes(hx[rows, :])
            total = 0.0
            for q in range(3):
                total = total + fw[2 * q, rows, :] * near[4 * q]
                total = total + fw[2 * q + 1, rows, :] * jnp.where(below, near[4 * q + 2], near[4 * q - 2])
            fx[rows, :] = swap_sides(total)

    with jax.named_scope("chain"):
        moa[...] = jnp.zeros_like(moa)
        mia[...] = jnp.zeros_like(mia)

        @pl.loop(0, NR // 2, unroll=8)
        def _(i):
            column = iota((CH, NC), 1)
            outer = (column == 0) | (column == NC - 1)
            hidden = []
            for k in range(4):
                add = jnp.where(outer, pltpu.roll(fx[...], NC - 1 - 8 * i - 2 * k, axis=1), 0.0)
                hidden.append((hid[i, :, NC * k : NC * (k + 1)] + add).astype(BF16))
            hidden = jnp.concatenate(hidden, axis=1)
            shift = w[27]
            pre = dot(mi[...], hidden) + jnp.concatenate([shift] * 4, axis=1)
            cdf = 0.5 * (1.0 + lax.erf(pre * INV_SQRT2))
            dens = jnp.exp(-0.5 * pre * pre) * INV_SQRT2PI
            act = (pre * cdf).astype(BF16)
            pg = (dot(mot[...], cb[i]) * (cdf + pre * dens)).astype(BF16)
            moa[...] += dot_nt(cb[i], act)
            mia[...] += dot_nt(pg, jnp.concatenate([hidden, jnp.ones((16, 4 * NC), BF16)], axis=0))
            pgs[i] = pg

    def over_sx(src, dst, sends, recvs, d):
        return pltpu.make_async_remote_copy(
            src_ref=src, dst_ref=dst.at[sx], send_sem=sends.at[d], recv_sem=recvs.at[sx],
            device_id=around(d, 0), device_id_type=MESH,
        )

    def over_group(src, dst, sends, recvs, d):
        return pltpu.make_async_remote_copy(
            src_ref=src, dst_ref=dst.at[me], send_sem=sends.at[d], recv_sem=recvs.at[me],
            device_id=at_group(lax.rem(me + d, n_group)), device_id_type=MESH,
        )

    def scatter(d):
        return over_sx(gs.at[lax.rem(sx + d, n_sx)], ar, asend, arecv, d)

    def publish(d):
        return over_sx(fo, fin, csend, crecv, d)

    def arrived(ref, sem, slot):
        pltpu.make_async_remote_copy(
            src_ref=ref.at[slot], dst_ref=ref.at[slot], send_sem=asend.at[0], recv_sem=sem.at[slot],
            device_id=around(1, 0), device_id_type=MESH,
        ).wait_recv()

    def arrived_sx(ref, sem):
        for d in range(1, n_sx):
            arrived(ref, sem, lax.rem(sx + d, n_sx))

    def arrived_group(ref, sem):
        for d in range(1, n_group):
            arrived(ref, sem, lax.rem(me + d, n_group))

    def added(ref, count):
        total = ref[0].astype(F32)
        for k in range(1, count):
            total = total + ref[k].astype(F32)
        return total

    def own_mixes():
        return pltpu.make_async_copy(fo, fin.at[sx], save.at[3])

    def own_taps():
        return pltpu.make_async_copy(kt, kg.at[me], save.at[4])

    def sum_sx():
        if comm:
            arrived_sx(ar, arecv)
            ar[sx] = gs[sx]
            bs[...] = added(ar, n_sx).astype(BF16)
            for d in range(1, n_group):
                over_group(bs, br, bsend, brecv, d).start()
            br[me] = bs[...]

    def sum_group():
        if comm:
            arrived_group(br, brecv)
            fo[...] = added(br, n_group).astype(BF16)
            for d in range(1, n_sx):
                publish(d).start()
            own_mixes().start()

    def sum_taps():
        if comm:
            arrived_sx(kr, krecv)
            kr[sx] = ks[...]
            kt[...] = added(kr, n_sx).astype(BF16)
            for d in range(1, n_group):
                over_group(kt, kg, lsend, lrecv, d).start()
            own_taps().start()

    with jax.named_scope("scatter mixes"):
        for k in range(PARTS):
            at = pl.ds(24 * k, 24)
            mid = jnp.concatenate([moa[at, 128:192], mia[at, 0:64]], axis=1)
            value = jnp.concatenate([moa[at, 0:128], mid, mia[at, 64:192], jnp.zeros((8, 128), F32)], axis=0)
            gs[k] = value.astype(BF16)
        if comm:
            for d in range(1, n_sx):
                scatter(d).start()

    with jax.named_scope("hidden grad"):
        @pl.loop(0, NR // 2, unroll=8)
        def _(i):
            hg = dot(mit[...], pgs[i]).astype(BF16)
            for k in range(4):
                piece = hg[:, NC * k : NC * (k + 1)]
                hb[2 * i + 1 + k // 2, k % 2] = piece
                b0[2 * i + 1 + k // 2, k % 2] = piece.astype(F32)
            edge[i] = dot_nt(pick_matrix(), hg)

    with jax.named_scope("send grad"):
        if comm:
            for k in range(3):
                slab_copy(1, hb, 0, k).start()
                slab_copy(1, hb, 1, k).start()
        pack_edges(ph)
        send_edges(1, ph, prh)

    def tap_sums(start, stop):
        @pl.loop(start, stop)
        def _(b):
            rows = block_of(b, BLK)
            for k, value in enumerate(tap_sums_block(b0, a0, am, ap, hx, gp, rows)):
                acc[k, rows, :] = value

    with jax.named_scope("tap sums"):
        gp[...] = swap_sides(edge_lanes())
        tap_sums(0, 16)
    with jax.named_scope("sum sx"):
        sum_sx()
    with jax.named_scope("tap sums 2"):
        tap_sums(16, 24)
        acc[27] = jnp.where(iota((CH, NC), 1) == 0, mia[:, 192:193], 0.0)

        for k in range(28):
            value = acc[k]
            high = value.astype(BF16)
            low = (value - high.astype(F32)).astype(BF16)
            flat[k] = dot_nt(jnp.ones((8, 2 * NC), BF16), jnp.concatenate([high, low], axis=1))

    with jax.named_scope("scatter taps"):
        value = jnp.concatenate([flat[k, 0:1] for k in range(28)] + [jnp.zeros((4, CH), F32)], axis=0)
        ks[0:32] = value[:, 0:128].astype(BF16)
        ks[32:48] = jnp.concatenate([value[0:16, 128:192], value[16:32, 128:192]], axis=1).astype(BF16)
        if comm:
            for d in range(1, n_sx):
                over_sx(ks, kr, ksend, krecv, d).start()

    with jax.named_scope("spread grad"):
        spread_all(1, hb, b0, bm, bp, ph, prh)

    def input_grad(start, stop):
        @pl.loop(2 * start, 2 * stop)
        def _(b):
            rows = block_of(b, BLK)

            def emit(i, first, second):
                at = 256 * (i % 2)
                ag[i // 2, rows, at : at + 128] = first
                ag[i // 2, rows, at + 128 : at + 256] = second

            stencil_block(b0, bm, bp, w, True, rows, emit)

        @pl.loop(start, stop, unroll=stop - start)
        def _(b):
            rows = block_of(b, WIDE)
            rhs = [ag[i // 2, rows, 256 * (i % 2) : 256 * (i % 2) + 256].astype(BF16) for i in range(NR)]
            both = dot(swap[...], jnp.concatenate(rhs, axis=0))
            for z in range(2):
                value = both[:, NC * z : NC * (z + 1)].reshape(WIDE, NR, NC)
                ov[rows, z] = (cv[rows, z].astype(F32) + value).astype(BF16)

    def save_part(part):
        at = pl.ds(third * part, third)
        return pltpu.make_async_copy(ov.at[at], ig_hbm.at[at], save.at[part])

    with jax.named_scope("grad 1"):
        input_grad(0, 3)
    with jax.named_scope("sum rest"):
        sum_taps()
    with jax.named_scope("grad 2"):
        input_grad(3, 5)
    with jax.named_scope("sum rest 2"):
        sum_group()
    with jax.named_scope("grad 3"):
        input_grad(5, 8)
    save_part(0).start()
    save_part(1).start()
    with jax.named_scope("grad 4"):
        input_grad(8, 12)
    save_part(2).start()

    with jax.named_scope("finish"):
        if comm:
            for which, rows_ref, sent, recv in ((0, xb, px, prx), (1, hb, ph, prh)):
                for slot in range(6):
                    pack_copy(which, sent, recv, slot).wait_send()
                for k in range(3):
                    slab_copy(which, rows_ref, 0, k).wait_send()
                    slab_copy(which, rows_ref, 1, k).wait_send()
            for d in range(1, n_sx):
                scatter(d).wait_send()
                over_sx(ks, kr, ksend, krecv, d).wait_send()
                publish(d).wait_send()
            for d in range(1, n_group):
                over_group(bs, br, bsend, brecv, d).wait_send()
                over_group(kt, kg, lsend, lrecv, d).wait_send()
            arrived_sx(fin, crecv)
            arrived_group(kg, lrecv)
            own_mixes().wait()
            own_taps().wait()
        for part in range(3):
            save_part(part).wait()


def deliver(factor, n_group, ig_in, fin_in, kg_in, ig_out, kg_out, mig_out, bg_out, mog_out, held, fin, taps, kg, mig, bg, mog, sems):
    parts = CH // 4
    at = [pl.ds(parts * k, parts) for k in range(4)]
    inward = [pltpu.make_async_copy(ig_in.at[at[k]], held.at[at[k]], sems.at[0, k]) for k in range(4)]
    outward = [pltpu.make_async_copy(held.at[at[k]], ig_out.at[at[k]], sems.at[1, k]) for k in range(4)]
    first = pltpu.make_async_copy(fin_in, fin, sems.at[0, 4])
    second = pltpu.make_async_copy(kg_in, taps, sems.at[0, 5])
    first.start()
    second.start()
    for copy in inward:
        copy.start()
    first.wait()
    for k in range(PARTS):
        rows = pl.ds(24 * k, 24)
        value = fin[k].astype(F32) * factor
        mog[rows, 0:128] = value[0:24]
        mog[rows, 128:192] = value[24:48, 0:64]
        mig[rows, 0:64] = value[24:48, 64:128]
        mig[rows, 64:192] = value[48:72]
    second.wait()
    value = taps[0].astype(F32)
    for g in range(1, n_group):
        value = value + taps[g].astype(F32)
    value = value * factor
    kg[:, 0:128] = value[0:27]
    kg[0:16, 128:192] = value[32:48, 0:64]
    kg[16:27, 128:192] = value[32:43, 64:128]
    bg[:, 0:128] = value[27:28]
    bg[:, 128:192] = value[43:44, 64:128]
    pairs = ((kg, kg_out), (mig, mig_out), (bg, bg_out), (mog, mog_out))
    small = [pltpu.make_async_copy(src, dst, sems.at[1, 4 + k]) for k, (src, dst) in enumerate(pairs)]
    for copy in small:
        copy.start()
    for k in range(4):
        inward[k].wait()
        outward[k].start()
    for copy in outward + small:
        copy.wait()


def per_device(sizes, factor, inputs, cotangent, depth_kernel, mix_in, mix_bias, mix_out):
    tile = (CH, 2, NR, NC)
    vm = pltpu.VMEM
    field = (RR, 2, CH, NC)
    pairs = (NR // 2, CH, 4 * NC)
    dma = pltpu.SemaphoreType.DMA
    n_sx, n_sy, n_sample = sizes
    mixes = (PARTS, PIECE, 128)
    taps = (16, CHUNK, 128)
    scratch = [
        vm(tile, BF16), vm(tile, BF16), vm(tile, BF16),
        vm((27, CH), F32), vm((1, CH), F32), vm((CH, CH), BF16), vm((CH, CH), BF16),
        vm(field, BF16), vm(field, BF16),
        vm(field, F32), vm(field, F32), vm(field, F32),
        vm(field, F32), vm(field, F32), vm(field, F32),
        vm(pairs, BF16), vm(pairs, F32), vm(pairs, F32),
        vm((28, CH, 128), F32), vm((28, CH, 128), F32),
        vm((CH, CH), BF16), vm((CH, CH), BF16), vm((NC, 2 * NC), BF16), vm((256, 256), BF16),
        vm((4, 16, CH), BF16), vm((4, 16, CH), BF16), vm((6, 4, 16, CH), BF16), vm((6, 4, 16, CH), BF16),
        vm((NR // 2, 8, CH), F32), vm((CH, 128), BF16),
        vm((CH, 128), F32), vm((CH, 128), F32), vm((CH, 128), F32), vm((6, CH, 128), F32),
        vm((CH, CH), F32), vm((CH, CH + 16), F32), vm((CH, 128), BF16), vm((28, 8, CH), F32),
        vm((PARTS, PIECE, 128), BF16), vm((PARTS, PIECE, 128), BF16), vm((16, PIECE, 128), BF16),
        vm((PIECE, 128), BF16), vm((PIECE, 128), BF16), vm(pairs, BF16),
        vm((CHUNK, 128), BF16), vm((8, CHUNK, 128), BF16), vm((CHUNK, 128), BF16),
        dma((8,)), dma((5,)), dma((2, 12)), dma((2, 12)),
        dma((8,)), dma((8,)), dma((16,)), dma((16,)), dma((8,)), dma((8,)),
        dma((8,)), dma((8,)), dma((16,)), dma((16,)),
    ]
    there = pl.BlockSpec(memory_space=pl.ANY)
    params = dict(vmem_limit_bytes=60 * 1024 * 1024)
    if n_sx > 1:
        params.update(collective_id=0, has_side_effects=True)
    ig, fin, kg = pl.pallas_call(
        functools.partial(kernel, sizes),
        out_shape=tuple(jax.ShapeDtypeStruct(shape, BF16) for shape in (tile, mixes, taps)),
        in_specs=[there] * 6,
        out_specs=(there,) * 3,
        scratch_shapes=scratch,
        compiler_params=pltpu.CompilerParams(**params),
        name="block",
    )(
        inputs.reshape(tile),
        cotangent.reshape(tile),
        depth_kernel.T,
        mix_bias.reshape(1, CH),
        mix_in,
        mix_out,
    )
    ig, kg, mig, bg, mog = pl.pallas_call(
        functools.partial(deliver, factor, n_sy * n_sample),
        out_shape=(
            jax.ShapeDtypeStruct(tile, BF16),
            jax.ShapeDtypeStruct((27, CH), F32),
            jax.ShapeDtypeStruct((CH, CH), F32),
            jax.ShapeDtypeStruct((1, CH), F32),
            jax.ShapeDtypeStruct((CH, CH), F32),
        ),
        in_specs=[there] * 3,
        out_specs=(there,) * 5,
        scratch_shapes=[
            vm(tile, BF16), vm(mixes, BF16), vm(taps, BF16), vm((27, CH), F32), vm((CH, CH), F32), vm((1, CH), F32),
            vm((CH, CH), F32), dma((2, 8)),
        ],
        compiler_params=pltpu.CompilerParams(vmem_limit_bytes=60 * 1024 * 1024),
        name="deliver",
    )(ig, fin, kg)
    return (ig.reshape(inputs.shape), kg.T, mig, bg.reshape(CH), mog)


def solution(mesh):
    sizes = tuple(mesh.shape[a] for a in ("sx", "sy", "sample"))
    cells = sizes[0] * sizes[1] * sizes[2] * 2 * NR * NC
    field = P("sample", None, None, "sx", "sy")
    return jax.shard_map(
        functools.partial(per_device, sizes, 1.0 / math.sqrt(cells)),
        mesh=mesh,
        in_specs=(field, field, P(), P(), P(), P()),
        out_specs=(field, P(), P(), P(), P()),
        check_vma=False,
    )
```

```python
import functools
import math

import jax
import jax.numpy as jnp
from jax import lax
from jax.experimental import pallas as pl
from jax.experimental.pallas import tpu as pltpu
from jax.sharding import PartitionSpec as P

INV_SQRT2 = 0.7071067811865476
INV_SQRT2PI = 0.3989422804014327
MESH = pl.DeviceIdType.MESH
F32 = jnp.float32
BF16 = jnp.bfloat16

CH = 192
NR = 16
NC = 128
RR = NR + 2
BLK = 8
WIDE = 16
CHUNK = 48
PIECE = 80
PARTS = 8


def dot(a, b):
    return jnp.dot(a, b, preferred_element_type=F32)


def dot_nt(a, b):
    return lax.dot_general(a, b, (((1,), (1,)), ((), ())), preferred_element_type=F32)


def iota(shape, dim):
    return lax.broadcasted_iota(jnp.int32, shape, dim)


def one_hot(cond):
    return jnp.where(cond, 1.0, 0.0).astype(BF16)


def block_of(b, size):
    return pl.ds(pl.multiple_of(b * size, size), size)


def rim_place(r, z):
    return 4 * r + 2 * z


def swap_sides(packed):
    even = iota(packed.shape, 1) % 2 == 0
    return jnp.where(even, pltpu.roll(packed, 127, axis=1), pltpu.roll(packed, 1, axis=1))


def pick_matrix():
    u = iota((8, 4 * NC), 0)
    k = iota((8, 4 * NC), 1)
    return one_hot(k == (u // 2) * NC + jnp.where(u % 2 == 0, NC - 1, 0))


def rim_matrix(at):
    lane = iota((128, 2 * NC), 0)
    j = iota((128, 2 * NC), 1)
    return one_hot(((j == 0) & (lane == at)) | ((j == 2 * NC - 1) & (lane == at + 1)))


def shift_matrix():
    k = iota((NC, 2 * NC), 0)
    j = iota((NC, 2 * NC), 1)
    return one_hot(((j < NC) & (k == j - 1)) | ((j >= NC) & (k == j - NC + 1)))


def swap_matrix():
    k = iota((256, 256), 0)
    j = iota((256, 256), 1)
    return one_hot((k // 16 == j % 16) & (k % 16 == j // 16))


def tap_matrix(d):
    row = iota((128, 256), 0)
    k = jnp.where(row < 96, row % 32, -2)
    t = 2 * d + jnp.where(iota((128, 256), 1) < 128, 0, 1)
    plus = jnp.where(t < 9, t + 9, jnp.where(t < 18, t + 9, jnp.where(t < 27, t - 18, 27)))
    minus = jnp.where((t < 9) | (t > 26), -1, jnp.where(t < 18, t, t - 9))
    return (jnp.where(k == plus, 1.0, 0.0) - jnp.where(k == minus, 1.0, 0.0)).astype(BF16)


def stencil_block(a0, am, ap, w, flip, rows, emit, first_row=0, last_row=RR - 1):
    k0 = [w[8 - t if flip else t, rows, :] for t in range(9)]
    kp = [w[18 + 8 - t if flip else 9 + t, rows, :] for t in range(9)]
    km = [w[9 + 8 - t if flip else 18 + t, rows, :] for t in range(9)]
    live = {}
    for r in range(first_row, last_row + 1):
        lower = [ref[r, 0, rows, :] for ref in (am, a0, ap)]
        upper = [ref[r, 1, rows, :] for ref in (am, a0, ap)]
        both = [u + v for u, v in zip(lower, upper)]
        for q in (1, 0, -1):
            i = r - 1 - q
            if not 0 <= i < NR:
                continue
            total = live.get(i, [None, None, None])
            for s in range(3):
                t = 3 * (q + 1) + s
                terms = (k0[t] * both[s], kp[t] * upper[s], km[t] * lower[s])
                total = [b if a is None else a + b for a, b in zip(total, terms)]
            live[i] = total
        for i in sorted(live):
            if i + 2 == r or r == last_row:
                shared, first, second = live.pop(i)
                emit(i, shared + first, shared + second)


def near_lanes(packed):
    return {off: pltpu.roll(packed, (128 - off) % 128, axis=1) if off else packed for off in range(-2, 12, 2)}


def tap_sums_block(g0, a0, am, ap, hx, gp, rows):
    near = near_lanes(hx[rows, :])
    grads = gp[rows, :]
    lane = iota((BLK, NC), 1)
    even = lane % 2 == 0
    lower_grads = jnp.where(lane % 4 < 2, grads, 0.0)
    upper_grads = grads - lower_grads
    sums = [jnp.zeros((BLK, NC), F32)] * 27
    for q in range(3):
        up = lower_grads * near[4 * q + 2]
        down = upper_grads * near[4 * q - 2]
        for kind, value in ((0, grads * near[4 * q] + up + down), (1, up), (2, down)):
            left = jnp.where(even, value, 0.0)
            sums[9 * kind + 3 * q] = left
            sums[9 * kind + 3 * q + 2] = value - left

    def step(r, sums):
        sums = list(sums)
        first = g0[r + 1, 0, rows, :]
        second = g0[r + 1, 1, rows, :]
        shared = first + second
        for q in range(3):
            for s, ref in enumerate((am, a0, ap)):
                lower = ref[r + q, 0, rows, :]
                upper = ref[r + q, 1, rows, :]
                t = 3 * q + s
                sums[t] = sums[t] + shared * (lower + upper)
                sums[9 + t] = sums[9 + t] + first * upper
                sums[18 + t] = sums[18 + t] + second * lower
        return tuple(sums)

    sums = lax.fori_loop(0, NR, step, tuple(sums), unroll=8)
    middle = [sums[t] - sums[9 + t] - sums[18 + t] for t in range(9)]
    return list(sums[18:]) + middle + list(sums[9:18])


def kernel(
    sizes,
    x_hbm, cot_hbm, dk_hbm, bias_hbm, mi_hbm, mo_hbm,
    ig_hbm, fin, kg,
    xv, cv, ov, dk, bias, mi, mo,
    xb, hb, a0, am, ap, b0, bm, bp, cb, ag, hid, w, acc, mit, mot, turn, swap,
    px, ph, prx, prh, edge, halo, hx, fx, gp, fw, moa, mia, tall, flat, gs, ar, br, fo, bs, pgs, ks, kr, kt,
    load, save, hsend, hrecv, asend, arecv, bsend, brecv, csend, crecv, ksend, krecv, lsend, lrecv,
):
    n_sx, n_sy, n_sample = sizes
    comm = n_sx > 1
    n_group = n_sy * n_sample
    sx, sy, sample = (lax.axis_index(a) for a in ("sx", "sy", "sample"))
    me = sy * n_sample + sample

    def at_group(g):
        return {"sx": sx, "sy": g // n_sample, "sample": g % n_sample}

    def around(dx, dy):
        return {
            "sx": lax.rem(sx + dx + n_sx, n_sx),
            "sy": lax.rem(sy + dy + n_sy, n_sy),
            "sample": sample,
        }

    third = CH // 3
    loads = [pltpu.make_async_copy(x_hbm.at[pl.ds(third * k, third)], xv.at[pl.ds(third * k, third)], load.at[k]) for k in range(3)]
    loads += [
        pltpu.make_async_copy(src, dst, load.at[3 + k])
        for k, (src, dst) in enumerate(((mi_hbm, mi), (mo_hbm, mo), (dk_hbm, dk), (bias_hbm, bias), (cot_hbm, cv)))
    ]
    with jax.named_scope("start"):
        for copy in loads[3:7] + loads[:3]:
            copy.start()
        if comm:
            barrier = pltpu.get_barrier_semaphore()
            for d in range(1, n_group):
                pl.semaphore_signal(barrier, inc=1, device_id=at_group(lax.rem(me + d, n_group)), device_id_type=MESH)
            for d in range(1, n_sx):
                pl.semaphore_signal(barrier, inc=1, device_id=around(d, 0), device_id_type=MESH)
            for dx in (-1, 1):
                for dy in (-1, 1):
                    pl.semaphore_signal(barrier, inc=1, device_id=around(dx, dy), device_id_type=MESH)

    pack_to = ((0, 1, 0), (1, 1, 1), (-1, 1, 2), (0, -1, 3), (1, -1, 4), (-1, -1, 5))

    def pack_copy(which, src, dst, slot):
        dx, dy, at = pack_to[slot]
        if dx:
            src, dst = src.at[3 if dx > 0 else 0], dst.at[at, 0]
        else:
            dst = dst.at[at]
        return pltpu.make_async_remote_copy(
            src_ref=src, dst_ref=dst, send_sem=hsend.at[which, at], recv_sem=hrecv.at[which, at],
            device_id=around(dx, dy), device_id_type=MESH,
        )

    def slab_copy(which, ref, up, k):
        part = pl.ds(third * k, third)
        return pltpu.make_async_remote_copy(
            src_ref=ref.at[NR if up else 1, :, part], dst_ref=ref.at[0 if up else NR + 1, :, part],
            send_sem=hsend.at[which, 6 + 3 * up + k], recv_sem=hrecv.at[which, 6 + 3 * up + k],
            device_id=around(1 if up else -1, 0), device_id_type=MESH,
        )

    def pack_edges(sent):
        for k in range(4):
            sent[k] = jnp.concatenate([edge[2 * k], edge[2 * k + 1]], axis=0).astype(BF16)

    def send_edges(which, sent, recv):
        if comm:
            for slot in range(6):
                pack_copy(which, sent, recv, slot).start()

    def rim(recv):
        def piece(slot, block, dx, dy):
            ok = (sx + dx >= 0) & (sx + dx < n_sx) & (sy + dy >= 0) & (sy + dy < n_sy)
            return jnp.where(ok, recv[slot, block].astype(F32), 0.0)

        left = iota((16, CH), 0) % 2 == 0
        tall = [jnp.where(left, piece(0, k, 0, -1), piece(3, k, 0, 1)) for k in range(4)]
        tall.append(jnp.where(left, piece(2, 0, 1, -1), piece(5, 0, 1, 1)))
        tall.append(jnp.zeros((32, CH), F32))
        tall.append(jnp.where(left, piece(1, 0, -1, -1), piece(4, 0, -1, 1)))
        square = jnp.concatenate(tall, axis=0)
        square = jnp.concatenate([square, jnp.zeros((128, 64), F32)], axis=1)
        return pltpu.roll(square.T[:CH], 4, axis=1)

    def edge_lanes():
        square = jnp.concatenate([edge[...].reshape(64, CH), jnp.zeros((64, CH), F32)], axis=0)
        square = jnp.concatenate([square, jnp.zeros((128, 64), F32)], axis=1)
        return square.T[:CH]

    def real_row(rows_ref, r):
        ok = sx > 0 if r == 0 else sx < n_sx - 1
        return jnp.where(ok, rows_ref[r].astype(F32), 0.0).astype(BF16)

    def spread_plain(value, mid, back, ahead, r):
        mid[r] = value.astype(F32)
        both = dot(value.reshape(2 * CH, NC), turn[...])
        back[r] = both[:, :NC].reshape(2, CH, NC)
        ahead[r] = both[:, NC:].reshape(2, CH, NC)

    def spread(rows_ref, mid, back, ahead, r, z):
        value = real_row(rows_ref, r)[z] if isinstance(r, int) else rows_ref[r, z]
        mid[r, z] = value.astype(F32)
        lhs = jnp.concatenate([value, halo[...]], axis=1)
        rhs = jnp.concatenate([turn[...], rim_matrix(rim_place(r, z))], axis=0)
        both = dot(lhs, rhs)
        back[r, z] = both[:, :NC]
        ahead[r, z] = both[:, NC:]

    def spread_all(which, rows_ref, mid, back, ahead, sent, recv):
        if comm:
            for slot in range(6):
                pack_copy(which, sent, recv, slot).wait_recv()
            halo[...] = rim(recv).astype(BF16)
        else:
            halo[...] = jnp.zeros_like(halo)

        @pl.loop(1, NR + 1, unroll=4)
        def _(r):
            for z in range(2):
                spread(rows_ref, mid, back, ahead, r, z)

        if comm:
            for k in range(3):
                slab_copy(which, rows_ref, 0, k).wait_recv()
                slab_copy(which, rows_ref, 1, k).wait_recv()
        else:
            rows_ref[0] = jnp.zeros_like(rows_ref[0])
            rows_ref[NR + 1] = jnp.zeros_like(rows_ref[0])
        for r in (0, NR + 1):
            for z in range(2):
                spread(rows_ref, mid, back, ahead, r, z)

    with jax.named_scope("constants"):
        for k in range(3, 7):
            loads[k].wait()
        turn[...] = shift_matrix()
        swap[...] = swap_matrix()
        eye = one_hot(iota((CH, CH), 0) == iota((CH, CH), 1))
        mit[...] = dot_nt(eye, mi[...]).astype(BF16)
        mot[...] = dot_nt(eye, mo[...]).astype(BF16)

    with jax.named_scope("weights"):
        value = jnp.concatenate([dk[...], bias[...], jnp.zeros((100, CH), F32)], axis=0)
        value = jnp.concatenate([value, jnp.zeros((128, 64), F32)], axis=1).T[:CH]
        high = value.astype(BF16).astype(F32)
        middle = (value - high).astype(BF16).astype(F32)
        low = value - high - middle
        tall[...] = (high + pltpu.roll(middle, 32, axis=1) + pltpu.roll(low, 64, axis=1)).astype(BF16)

        @pl.loop(0, 14, unroll=7)
        def _(d):
            both = dot(tall[...], tap_matrix(d))
            w[2 * d] = both[:, :128]
            w[2 * d + 1] = both[:, 128:]

        even = iota((CH, 128), 1) % 2 == 0
        below = iota((CH, 128), 1) % 4 < 2
        for q in range(3):
            own, up, down = (jnp.where(even, w[9 * k + 3 * q], w[9 * k + 3 * q + 2]) for k in range(3))
            fw[2 * q] = own
            fw[2 * q + 1] = own + jnp.where(below, up, down)

    with jax.named_scope("rows of x"):
        for k in range(3):
            loads[k].wait()

            @pl.loop(4 * k, 4 * k + 4, unroll=4)
            def _(b):
                part = xv[block_of(b, WIDE)]
                rhs = jnp.concatenate([part[:, z].reshape(WIDE * NR, NC) for z in range(2)], axis=1)
                both = dot(swap[...], rhs).astype(BF16)
                for i in range(NR):
                    for z in range(2):
                        xb[i + 1, z, block_of(b, WIDE), :] = both[WIDE * i : WIDE * (i + 1), NC * z : NC * (z + 1)]

            if comm:
                if k == 0:
                    pl.semaphore_wait(barrier, n_group - 1 + n_sx - 1 + 4)
                slab_copy(0, xb, 0, k).start()
                slab_copy(0, xb, 1, k).start()
        loads[7].start()

    with jax.named_scope("send x"):
        pick = pick_matrix()
        for i in range(NR // 2):
            four = jnp.concatenate([xb[2 * i + 1 + k // 2, k % 2] for k in range(4)], axis=1)
            edge[i] = dot_nt(pick, four)
        pack_edges(px)
        send_edges(0, px, prx)

    with jax.named_scope("spread x"):
        @pl.loop(1, NR + 1, unroll=8)
        def _(r):
            spread_plain(xb[r], a0, am, ap, r)

    loads[7].wait()
    with jax.named_scope("cotangent"):
        @pl.loop(0, CH // WIDE, unroll=12)
        def _(b):
            part = cv[block_of(b, WIDE)]
            rhs = jnp.concatenate([part[:, z].reshape(WIDE * NR, NC) for z in range(2)], axis=1)
            both = dot(swap[...], rhs).astype(BF16)
            for i in range(NR):
                cb[i // 2, block_of(b, WIDE), 256 * (i % 2) : 256 * (i % 2) + 256] = both[WIDE * i : WIDE * (i + 1)]

    with jax.named_scope("hidden"):
        @pl.loop(0, CH // BLK, unroll=2)
        def _(b):
            rows = block_of(b, BLK)

            def emit(i, first, second):
                at = 256 * (i % 2)
                hid[i // 2, rows, at : at + 128] = first
                hid[i // 2, rows, at + 128 : at + 256] = second

            stencil_block(a0, am, ap, w, False, rows, emit, 1, NR)

    with jax.named_scope("halo x"):
        if comm:
            for slot in range(6):
                pack_copy(0, px, prx, slot).wait_recv()
            hx[...] = rim(prx)
            for k in range(3):
                slab_copy(0, xb, 0, k).wait_recv()
                slab_copy(0, xb, 1, k).wait_recv()
        else:
            hx[...] = jnp.zeros_like(hx)
            xb[0] = jnp.zeros_like(xb[0])
            xb[NR + 1] = jnp.zeros_like(xb[0])
        for r in (0, NR + 1):
            spread_plain(real_row(xb, r), a0, am, ap, r)

        @pl.loop(0, CH // BLK, unroll=8)
        def _(b):
            rows = block_of(b, BLK)
            for r, i, t0 in ((0, 0, 0), (NR + 1, NR - 1, 6)):
                shared, first, second = 0.0, 0.0, 0.0
                for s, ref in enumerate((am, a0, ap)):
                    lower = ref[r, 0, rows, :]
                    upper = ref[r, 1, rows, :]
                    shared = shared + w[t0 + s, rows, :] * (lower + upper)
                    first = first + w[9 + t0 + s, rows, :] * upper
                    second = second + w[18 + t0 + s, rows, :] * lower
                at = 256 * (i % 2)
                hid[i // 2, rows, at : at + 128] += shared + first
                hid[i // 2, rows, at + 128 : at + 256] += shared + second

            below = iota((BLK, 128), 1) % 4 < 2
            near = near_lanes(hx[rows, :])
            total = 0.0
            for q in range(3):
                total = total + fw[2 * q, rows, :] * near[4 * q]
                total = total + fw[2 * q + 1, rows, :] * jnp.where(below, near[4 * q + 2], near[4 * q - 2])
            fx[rows, :] = swap_sides(total)

    with jax.named_scope("chain"):
        moa[...] = jnp.zeros_like(moa)
        mia[...] = jnp.zeros_like(mia)

        @pl.loop(0, NR // 2, unroll=8)
        def _(i):
            column = iota((CH, NC), 1)
            outer = (column == 0) | (column == NC - 1)
            hidden = []
            for k in range(4):
                add = jnp.where(outer, pltpu.roll(fx[...], NC - 1 - 8 * i - 2 * k, axis=1), 0.0)
                hidden.append((hid[i, :, NC * k : NC * (k + 1)] + add).astype(BF16))
            hidden = jnp.concatenate(hidden, axis=1)
            shift = w[27]
            pre = dot(mi[...], hidden) + jnp.concatenate([shift] * 4, axis=1)
            cdf = 0.5 * (1.0 + lax.erf(pre * INV_SQRT2))
            dens = jnp.exp(-0.5 * pre * pre) * INV_SQRT2PI
            act = (pre * cdf).astype(BF16)
            pg = (dot(mot[...], cb[i]) * (cdf + pre * dens)).astype(BF16)
            moa[...] += dot_nt(cb[i], act)
            mia[...] += dot_nt(pg, jnp.concatenate([hidden, jnp.ones((16, 4 * NC), BF16)], axis=0))
            pgs[i] = pg

    def over_sx(src, dst, sends, recvs, d):
        return pltpu.make_async_remote_copy(
            src_ref=src, dst_ref=dst.at[sx], send_sem=sends.at[d], recv_sem=recvs.at[sx],
            device_id=around(d, 0), device_id_type=MESH,
        )

    def over_group(src, dst, sends, recvs, d):
        return pltpu.make_async_remote_copy(
            src_ref=src, dst_ref=dst.at[me], send_sem=sends.at[d], recv_sem=recvs.at[me],
            device_id=at_group(lax.rem(me + d, n_group)), device_id_type=MESH,
        )

    def scatter(d):
        return over_sx(gs.at[lax.rem(sx + d, n_sx)], ar, asend, arecv, d)

    def publish(d):
        return over_sx(fo, fin, csend, crecv, d)

    def arrived(ref, sem, slot):
        pltpu.make_async_remote_copy(
            src_ref=ref.at[slot], dst_ref=ref.at[slot], send_sem=asend.at[0], recv_sem=sem.at[slot],
            device_id=around(1, 0), device_id_type=MESH,
        ).wait_recv()

    def arrived_sx(ref, sem):
        for d in range(1, n_sx):
            arrived(ref, sem, lax.rem(sx + d, n_sx))

    def arrived_group(ref, sem):
        for d in range(1, n_group):
            arrived(ref, sem, lax.rem(me + d, n_group))

    def added(ref, count):
        total = ref[0].astype(F32)
        for k in range(1, count):
            total = total + ref[k].astype(F32)
        return total

    def own_mixes():
        return pltpu.make_async_copy(fo, fin.at[sx], save.at[3])

    def own_taps():
        return pltpu.make_async_copy(kt, kg.at[me], save.at[4])

    def sum_sx():
        if comm:
            arrived_sx(ar, arecv)
            ar[sx] = gs[sx]
            bs[...] = added(ar, n_sx).astype(BF16)
            for d in range(1, n_group):
                over_group(bs, br, bsend, brecv, d).start()
            br[me] = bs[...]

    def sum_group():
        if comm:
            arrived_group(br, brecv)
            fo[...] = added(br, n_group).astype(BF16)
            for d in range(1, n_sx):
                publish(d).start()
            own_mixes().start()

    def sum_taps():
        if comm:
            arrived_sx(kr, krecv)
            kr[sx] = ks[...]
            kt[...] = added(kr, n_sx).astype(BF16)
            for d in range(1, n_group):
                over_group(kt, kg, lsend, lrecv, d).start()
            own_taps().start()

    with jax.named_scope("scatter mixes"):
        for k in range(PARTS):
            at = pl.ds(24 * k, 24)
            mid = jnp.concatenate([moa[at, 128:192], mia[at, 0:64]], axis=1)
            value = jnp.concatenate([moa[at, 0:128], mid, mia[at, 64:192], jnp.zeros((8, 128), F32)], axis=0)
            gs[k] = value.astype(BF16)
        if comm:
            for d in range(1, n_sx):
                scatter(d).start()

    with jax.named_scope("hidden grad"):
        @pl.loop(0, NR // 2, unroll=8)
        def _(i):
            hg = dot(mit[...], pgs[i]).astype(BF16)
            for k in range(4):
                piece = hg[:, NC * k : NC * (k + 1)]
                hb[2 * i + 1 + k // 2, k % 2] = piece
                b0[2 * i + 1 + k // 2, k % 2] = piece.astype(F32)
            edge[i] = dot_nt(pick_matrix(), hg)

    with jax.named_scope("send grad"):
        if comm:
            for k in range(3):
                slab_copy(1, hb, 0, k).start()
                slab_copy(1, hb, 1, k).start()
        pack_edges(ph)
        send_edges(1, ph, prh)

    def tap_sums(start, stop):
        @pl.loop(start, stop, unroll=2)
        def _(b):
            rows = block_of(b, BLK)
            for k, value in enumerate(tap_sums_block(b0, a0, am, ap, hx, gp, rows)):
                acc[k, rows, :] = value

    with jax.named_scope("tap sums"):
        gp[...] = swap_sides(edge_lanes())
        tap_sums(0, 16)
    with jax.named_scope("sum sx"):
        sum_sx()
    with jax.named_scope("tap sums 2"):
        tap_sums(16, 24)
        acc[27] = jnp.where(iota((CH, NC), 1) == 0, mia[:, 192:193], 0.0)

        for k in range(28):
            value = acc[k]
            high = value.astype(BF16)
            low = (value - high.astype(F32)).astype(BF16)
            flat[k] = dot_nt(jnp.ones((8, 2 * NC), BF16), jnp.concatenate([high, low], axis=1))

    with jax.named_scope("scatter taps"):
        value = jnp.concatenate([flat[k, 0:1] for k in range(28)] + [jnp.zeros((4, CH), F32)], axis=0)
        ks[0:32] = value[:, 0:128].astype(BF16)
        ks[32:48] = jnp.concatenate([value[0:16, 128:192], value[16:32, 128:192]], axis=1).astype(BF16)
        if comm:
            for d in range(1, n_sx):
                over_sx(ks, kr, ksend, krecv, d).start()

    with jax.named_scope("spread grad"):
        spread_all(1, hb, b0, bm, bp, ph, prh)

    def input_grad(start, stop):
        @pl.loop(2 * start, 2 * stop)
        def _(b):
            rows = block_of(b, BLK)

            def emit(i, first, second):
                at = 256 * (i % 2)
                ag[i // 2, rows, at : at + 128] = first
                ag[i // 2, rows, at + 128 : at + 256] = second

            stencil_block(b0, bm, bp, w, True, rows, emit)

        @pl.loop(start, stop, unroll=stop - start)
        def _(b):
            rows = block_of(b, WIDE)
            rhs = [ag[i // 2, rows, 256 * (i % 2) : 256 * (i % 2) + 256].astype(BF16) for i in range(NR)]
            both = dot(swap[...], jnp.concatenate(rhs, axis=0))
            for z in range(2):
                value = both[:, NC * z : NC * (z + 1)].reshape(WIDE, NR, NC)
                ov[rows, z] = (cv[rows, z].astype(F32) + value).astype(BF16)

    def save_part(part):
        at = pl.ds(third * part, third)
        return pltpu.make_async_copy(ov.at[at], ig_hbm.at[at], save.at[part])

    with jax.named_scope("grad 1"):
        input_grad(0, 3)
    with jax.named_scope("sum rest"):
        sum_taps()
    with jax.named_scope("grad 2"):
        input_grad(3, 5)
    with jax.named_scope("sum rest 2"):
        sum_group()
    with jax.named_scope("grad 3"):
        input_grad(5, 8)
    save_part(0).start()
    save_part(1).start()
    with jax.named_scope("grad 4"):
        input_grad(8, 12)
    save_part(2).start()

    with jax.named_scope("finish"):
        if comm:
            for which, rows_ref, sent, recv in ((0, xb, px, prx), (1, hb, ph, prh)):
                for slot in range(6):
                    pack_copy(which, sent, recv, slot).wait_send()
                for k in range(3):
                    slab_copy(which, rows_ref, 0, k).wait_send()
                    slab_copy(which, rows_ref, 1, k).wait_send()
            for d in range(1, n_sx):
                scatter(d).wait_send()
                over_sx(ks, kr, ksend, krecv, d).wait_send()
                publish(d).wait_send()
            for d in range(1, n_group):
                over_group(bs, br, bsend, brecv, d).wait_send()
                over_group(kt, kg, lsend, lrecv, d).wait_send()
            arrived_sx(fin, crecv)
            arrived_group(kg, lrecv)
            own_mixes().wait()
            own_taps().wait()
        for part in range(3):
            save_part(part).wait()


def deliver(factor, n_group, ig_in, fin_in, kg_in, ig_out, kg_out, mig_out, bg_out, mog_out, held, fin, taps, kg, mig, bg, mog, sems):
    parts = CH // 4
    at = [pl.ds(parts * k, parts) for k in range(4)]
    inward = [pltpu.make_async_copy(ig_in.at[at[k]], held.at[at[k]], sems.at[0, k]) for k in range(4)]
    outward = [pltpu.make_async_copy(held.at[at[k]], ig_out.at[at[k]], sems.at[1, k]) for k in range(4)]
    first = pltpu.make_async_copy(fin_in, fin, sems.at[0, 4])
    second = pltpu.make_async_copy(kg_in, taps, sems.at[0, 5])
    first.start()
    second.start()
    for copy in inward:
        copy.start()
    first.wait()
    for k in range(PARTS):
        rows = pl.ds(24 * k, 24)
        value = fin[k].astype(F32) * factor
        mog[rows, 0:128] = value[0:24]
        mog[rows, 128:192] = value[24:48, 0:64]
        mig[rows, 0:64] = value[24:48, 64:128]
        mig[rows, 64:192] = value[48:72]
    second.wait()
    value = taps[0].astype(F32)
    for g in range(1, n_group):
        value = value + taps[g].astype(F32)
    value = value * factor
    kg[:, 0:128] = value[0:27]
    kg[0:16, 128:192] = value[32:48, 0:64]
    kg[16:27, 128:192] = value[32:43, 64:128]
    bg[:, 0:128] = value[27:28]
    bg[:, 128:192] = value[43:44, 64:128]
    pairs = ((kg, kg_out), (mig, mig_out), (bg, bg_out), (mog, mog_out))
    small = [pltpu.make_async_copy(src, dst, sems.at[1, 4 + k]) for k, (src, dst) in enumerate(pairs)]
    for copy in small:
        copy.start()
    for k in range(4):
        inward[k].wait()
        outward[k].start()
    for copy in outward + small:
        copy.wait()


def per_device(sizes, factor, inputs, cotangent, depth_kernel, mix_in, mix_bias, mix_out):
    tile = (CH, 2, NR, NC)
    vm = pltpu.VMEM
    field = (RR, 2, CH, NC)
    pairs = (NR // 2, CH, 4 * NC)
    dma = pltpu.SemaphoreType.DMA
    n_sx, n_sy, n_sample = sizes
    mixes = (PARTS, PIECE, 128)
    taps = (16, CHUNK, 128)
    scratch = [
        vm(tile, BF16), vm(tile, BF16), vm(tile, BF16),
        vm((27, CH), F32), vm((1, CH), F32), vm((CH, CH), BF16), vm((CH, CH), BF16),
        vm(field, BF16), vm(field, BF16),
        vm(field, F32), vm(field, F32), vm(field, F32),
        vm(field, F32), vm(field, F32), vm(field, F32),
        vm(pairs, BF16), vm(pairs, F32), vm(pairs, F32),
        vm((28, CH, 128), F32), vm((28, CH, 128), F32),
        vm((CH, CH), BF16), vm((CH, CH), BF16), vm((NC, 2 * NC), BF16), vm((256, 256), BF16),
        vm((4, 16, CH), BF16), vm((4, 16, CH), BF16), vm((6, 4, 16, CH), BF16), vm((6, 4, 16, CH), BF16),
        vm((NR // 2, 8, CH), F32), vm((CH, 128), BF16),
        vm((CH, 128), F32), vm((CH, 128), F32), vm((CH, 128), F32), vm((6, CH, 128), F32),
        vm((CH, CH), F32), vm((CH, CH + 16), F32), vm((CH, 128), BF16), vm((28, 8, CH), F32),
        vm((PARTS, PIECE, 128), BF16), vm((PARTS, PIECE, 128), BF16), vm((16, PIECE, 128), BF16),
        vm((PIECE, 128), BF16), vm((PIECE, 128), BF16), vm(pairs, BF16),
        vm((CHUNK, 128), BF16), vm((8, CHUNK, 128), BF16), vm((CHUNK, 128), BF16),
        dma((8,)), dma((5,)), dma((2, 12)), dma((2, 12)),
        dma((8,)), dma((8,)), dma((16,)), dma((16,)), dma((8,)), dma((8,)),
        dma((8,)), dma((8,)), dma((16,)), dma((16,)),
    ]
    there = pl.BlockSpec(memory_space=pl.ANY)
    params = dict(vmem_limit_bytes=60 * 1024 * 1024)
    if n_sx > 1:
        params.update(collective_id=0, has_side_effects=True)
    ig, fin, kg = pl.pallas_call(
        functools.partial(kernel, sizes),
        out_shape=tuple(jax.ShapeDtypeStruct(shape, BF16) for shape in (tile, mixes, taps)),
        in_specs=[there] * 6,
        out_specs=(there,) * 3,
        scratch_shapes=scratch,
        compiler_params=pltpu.CompilerParams(**params),
        name="block",
    )(
        inputs.reshape(tile),
        cotangent.reshape(tile),
        depth_kernel.T,
        mix_bias.reshape(1, CH),
        mix_in,
        mix_out,
    )
    ig, kg, mig, bg, mog = pl.pallas_call(
        functools.partial(deliver, factor, n_sy * n_sample),
        out_shape=(
            jax.ShapeDtypeStruct(tile, BF16),
            jax.ShapeDtypeStruct((27, CH), F32),
            jax.ShapeDtypeStruct((CH, CH), F32),
            jax.ShapeDtypeStruct((1, CH), F32),
            jax.ShapeDtypeStruct((CH, CH), F32),
        ),
        in_specs=[there] * 3,
        out_specs=(there,) * 5,
        scratch_shapes=[
            vm(tile, BF16), vm(mixes, BF16), vm(taps, BF16), vm((27, CH), F32), vm((CH, CH), F32), vm((1, CH), F32),
            vm((CH, CH), F32), dma((2, 8)),
        ],
        compiler_params=pltpu.CompilerParams(vmem_limit_bytes=60 * 1024 * 1024),
        name="deliver",
    )(ig, fin, kg)
    return (ig.reshape(inputs.shape), kg.T, mig, bg.reshape(CH), mog)


def solution(mesh):
    sizes = tuple(mesh.shape[a] for a in ("sx", "sy", "sample"))
    cells = sizes[0] * sizes[1] * sizes[2] * 2 * NR * NC
    field = P("sample", None, None, "sx", "sy")
    return jax.shard_map(
        functools.partial(per_device, sizes, 1.0 / math.sqrt(cells)),
        mesh=mesh,
        in_specs=(field, field, P(), P(), P(), P()),
        out_specs=(field, P(), P(), P(), P()),
        check_vma=False,
    )
```
